128 devices in a mesh: dp: 32 (over y, x, core), section: 4 (over z).
Axes of the slice: x: 4, y: 4, z: 4, core: 2. Of those that a mesh axis runs over, the one named last changes fastest.
Arguments:
- inputs: bfloat16 [256, 128, 200], P('dp'), may hold values from -6 to 6
- lengths: int32 [256], P('dp'), may hold values from 1 to 128, as said below
- gene_mask: int32 [256, 128], P('dp'), may hold values from 0 to 1, as said below
- out_grad: float32 [256, 128, 200], P('dp'), may hold values from -6 to 6
- norm_gain: float32 [2, 2, 200], replicated, may hold values from 0.5 to 1.5
- norm_bias: float32 [2, 2, 200], replicated, may hold values from -1.75 to 1.75
- qkv_weight: bfloat16 [2, 200, 1920], replicated, may hold values from -0.3125 to 0.3125
- out_weight: bfloat16 [2, 640, 200], replicated, may hold values from -0.625 to 0.625
- out_bias: float32 [2, 200], replicated, may hold values from -1.75 to 1.75
- features: bfloat16 [2, 64, 266], replicated, may hold values from -6 to 6
- up_weight: bfloat16 [2, 200, 800], replicated, may hold values from -0.4375 to 0.4375
- up_bias: float32 [2, 800], replicated, may hold values from -1.75 to 1.75
- down_weight: bfloat16 [2, 800, 200], replicated, may hold values from -0.3125 to 0.3125
- down_bias: float32 [2, 200], replicated, may hold values from -1.75 to 1.75
Outputs:
- activations: float32 [4, 256, 128, 200], P('section', 'dp')
- stream_grads: float32 [4, 256, 128, 200], P('section', 'dp')
- grad_norm_gain: float32 [2, 2, 200], replicated
- grad_norm_bias: float32 [2, 2, 200], replicated
- grad_qkv_weight: float32 [2, 200, 1920], replicated
- grad_out_weight: float32 [2, 640, 200], replicated
- grad_out_bias: float32 [2, 200], replicated
- grad_up_weight: float32 [2, 200, 800], replicated
- grad_up_bias: float32 [2, 800], replicated
- grad_down_weight: float32 [2, 800, 200], replicated
- grad_down_bias: float32 [2, 200], replicated
The draws below stay inside these ranges and needn't reach their ends.
Inputs may be any that keep to these rules, and one draw needn't show every extreme that they name: `lengths`: some cell has exactly 128 expressed genes. `gene_mask`: the first slot of every cell is 1.
All inputs are finite; a program needn't handle non-finite values.
Results may differ from the reference program's by a relative error of at most 0.029.
Values sent between devices are 32-bit elements; how exact they have to be, the bound alone decides.
A program may use at most 192 MiB of HBM per device.

```python
import jax
import jax.numpy as jnp
from jax import lax

D = 200
HEADS = 10
HEAD_DIM = 64
FEATS = 266
FF = 800
LMAX = 128
INNER = 640
CELLS = 256
SUBLAYERS = 4
LAYERS = 2
N_DP = 32


def draw_lengths(key, part):
    key = jax.random.fold_in(key, 11)
    first_key, second_key, third_key = jax.random.split(key, 3)
    base = jax.random.randint(first_key, (CELLS,), 1, LMAX + 1)
    shrink = jax.random.randint(second_key, (CELLS,), 0, 4)
    counts = jnp.maximum(base // (1 + shrink * shrink), 1)
    longest = jax.random.randint(third_key, (), 0, CELLS)
    return jnp.where(jnp.arange(CELLS) == longest, LMAX, counts).astype(jnp.int32)


def draw_gene_mask(key, part):
    key = jax.random.fold_in(key, 23)
    values = jax.random.randint(key, (CELLS, LMAX), 0, 4)
    leading = jnp.arange(LMAX)[None, :] == 0
    return jnp.where(leading | (values > 0), 1, 0).astype(jnp.int32)


def block_levels(stream_key, dims, cuts, low, top_value):
    gain, own = 1.0, jax.random.fold_in(stream_key, 6)
    for axis_at, shards_of in cuts:
        draws = jnp.exp(jax.random.uniform(jax.random.fold_in(own, axis_at), (shards_of,), jnp.float32, low / len(cuts), top_value / len(cuts)))
        gain = gain * jnp.repeat(draws, dims[axis_at] // shards_of).reshape([-1 if axis == axis_at else 1 for axis in range(len(dims))])
    return gain


def gaussian(own_key, extent, width, most, shards=(), dtype=jnp.bfloat16):
    values = jax.random.normal(own_key, extent, jnp.float32) * width
    if len(shards) > 0:
        values = block_levels(own_key, extent, shards, -0.22, 0.18) * values
    return jnp.clip(values, min=-most, max=most).astype(dtype)


def setup_inputs(seed: int = 0) -> dict:
    key_list = jax.random.split(jax.random.key(seed), 15)
    inputs = gaussian(key_list[0], (CELLS, LMAX, D), 1.0, 6.0, ((0, 32),))
    lengths = draw_lengths(jax.random.fold_in(key_list[14], 71), 0)
    gene_mask = draw_gene_mask(jax.random.fold_in(key_list[14], 71), 0)
    out_grad = gaussian(key_list[3], (CELLS, LMAX, D), 1.0, 6.0, ((0, 32),), jnp.float32)
    norm_gain = jnp.clip(1.0 + 0.1 * jax.random.normal(key_list[4], (LAYERS, 2, D), jnp.float32), 0.5, 1.5)
    norm_bias = gaussian(key_list[5], (LAYERS, 2, D), 0.3, 1.75, (), jnp.float32)
    qkv_weight = gaussian(key_list[6], (LAYERS, D, 3 * INNER), (2 * D) ** -0.5, 0.3125)
    out_weight = gaussian(key_list[7], (LAYERS, INNER, D), (INNER // 8) ** -0.5, 0.625)
    out_bias = gaussian(key_list[8], (LAYERS, D), 0.3, 1.75, (), jnp.float32)
    features = gaussian(key_list[9], (LAYERS, HEAD_DIM, FEATS), 1.0, 6.0)
    up_weight = gaussian(key_list[10], (LAYERS, D, FF), D ** -0.5, 0.4375)
    up_bias = gaussian(key_list[11], (LAYERS, FF), 0.3, 1.75, (), jnp.float32)
    down_weight = gaussian(key_list[12], (LAYERS, FF, D), (FF // 2) ** -0.5, 0.3125)
    down_bias = gaussian(key_list[13], (LAYERS, D), 0.3, 1.75, (), jnp.float32)
    return {"inputs": inputs, "lengths": lengths, "gene_mask": gene_mask, "out_grad": out_grad, "norm_gain": norm_gain, "norm_bias": norm_bias, "qkv_weight": qkv_weight, "out_weight": out_weight, "out_bias": out_bias, "features": features, "up_weight": up_weight, "up_bias": up_bias, "down_weight": down_weight, "down_bias": down_bias}


EPSILON = 1e-05
ACCURATE = lax.Precision.HIGHEST

@jax.custom_vjp
def low(v):
    return lax.optimization_barrier(v.astype(jnp.bfloat16)).astype(jnp.float32)

@jax.custom_vjp
def low_back(v):
    return v

def low_keep(v):
    return (low(v), None)

def low_pass(kept, grad):
    return (grad,)

def back_keep(v):
    return (v, None)

def back_low(kept, grad):
    return (low(grad),)
low.defvjp(low_keep, low_pass)
low_back.defvjp(back_keep, back_low)

def rounded_both(tensor):
    return low_back(low(tensor))

def norm_apply(stream, gain_row, shift_row):
    centered = stream - lax.optimization_barrier(jnp.mean(stream, axis=-1, keepdims=True))
    normed = centered * lax.rsqrt(lax.optimization_barrier(jnp.mean(centered * centered, axis=-1, keepdims=True)) + EPSILON)
    return low(normed * gain_row + shift_row)

def feature_map(vectors, random_map, key_mask):
    logits = jnp.einsum('cnhe,ef->cnhf', vectors, random_map, precision=ACCURATE) * HEAD_DIM ** (-0.25)
    logits = low_back(logits - lax.optimization_barrier(jnp.sum(vectors * vectors, axis=-1, keepdims=True)) * (0.5 * HEAD_DIM ** (-0.5)))
    return low(jnp.exp(logits) * FEATS ** (-0.5)) * key_mask

def attention(stream, key_mask, gain_row, shift_row, qkv_mats, out_mats, out_shift, random_map):
    cell_count, slot_count, widths = stream.shape
    inner_width = HEADS * HEAD_DIM
    normed = norm_apply(stream, gain_row, shift_row)
    projected = jnp.einsum('cnd,dk->cnk', normed, qkv_mats, precision=ACCURATE)
    pieces = [rounded_both(projected[..., column_part * inner_width:(column_part + 1) * inner_width]).reshape(cell_count, slot_count, HEADS, HEAD_DIM) for column_part in range(3)]
    query_feat = feature_map(pieces[0], random_map, 1.0)
    key_feat = feature_map(pieces[1], random_map, key_mask[:, :, None, None])
    key_value = rounded_both(jnp.einsum('cnhf,cnhe->chfe', key_feat, pieces[2], precision=ACCURATE))
    key_total = lax.optimization_barrier(jnp.sum(key_feat, axis=1))
    numerator = low_back(jnp.einsum('cnhf,chfe->cnhe', query_feat, key_value, precision=ACCURATE))
    denominator = low_back(jnp.einsum('cnhf,chf->cnh', query_feat, key_total, precision=ACCURATE))
    attended = low((numerator / denominator[..., None]).reshape(cell_count, slot_count, inner_width))
    return low_back(jnp.einsum('cnd,de->cne', attended, out_mats, precision=ACCURATE) + out_shift)

def feed_forward(stream, gain_row, shift_row, up_mats, up_shift, down_mats, down_shift):
    normed = norm_apply(stream, gain_row, shift_row)
    before = low_back(jnp.einsum('cnd,df->cnf', normed, up_mats, precision=ACCURATE) + up_shift)
    hidden = low(jax.nn.gelu(before, approximate=False))
    return low_back(jnp.einsum('cnf,fd->cnd', hidden, down_mats, precision=ACCURATE) + down_shift)

def forward(probes, params, cell_block, key_mask, random_maps):
    gain_rows, shift_rows, qkv_mats, out_mats, out_shift, up_mats, up_shift, down_mats, down_shift = params
    stream = cell_block
    states = []
    for layer_index in range(LAYERS):
        stream = stream + probes[2 * layer_index]
        stream = stream + attention(stream, key_mask, gain_rows[layer_index, 0], shift_rows[layer_index, 0], qkv_mats[layer_index], out_mats[layer_index], out_shift[layer_index], random_maps[layer_index])
        states.append(stream)
        stream = stream + probes[2 * layer_index + 1]
        stream = stream + feed_forward(stream, gain_rows[layer_index, 1], shift_rows[layer_index, 1], up_mats[layer_index], up_shift[layer_index], down_mats[layer_index], down_shift[layer_index])
        states.append(stream)
    return (stream, jnp.stack(states))

def reference(inputs, lengths, gene_mask, out_grad, norm_gain, norm_bias, qkv_weight, out_weight, out_bias, features, up_weight, up_bias, down_weight, down_bias):
    random_maps = features.astype(jnp.float32)
    params = (norm_gain, norm_bias, qkv_weight.astype(jnp.float32), out_weight.astype(jnp.float32), out_bias, up_weight.astype(jnp.float32), up_bias, down_weight.astype(jnp.float32), down_bias)
    group_cells = CELLS // N_DP
    positions = lax.broadcasted_iota(jnp.int32, (CELLS, LMAX), 1)
    key_mask = jnp.where((positions < lengths[:, None]) & (gene_mask > 0), 1.0, 0.0).astype(jnp.float32)

    def regroup(tensor):
        return tensor.reshape((N_DP, group_cells) + tensor.shape[1:])

    def scan_step(totals, pieces):
        cell_block, block_mask, block_grad = pieces
        probes = jnp.zeros((SUBLAYERS,) + cell_block.shape, jnp.float32)

        def run_forward(probe_args, param_args):
            return forward(probe_args, param_args, cell_block, block_mask, random_maps)
        result, pull_back, states = jax.vjp(run_forward, probes, params, has_aux=True)
        probe_grads, param_grads = pull_back(block_grad)
        totals = jax.tree.map(lambda first, second: first + second, totals, param_grads)
        return (totals, (states, probe_grads))
    zero_sums = jax.tree.map(jnp.zeros_like, params)
    totals, (states, probe_grads) = lax.scan(scan_step, zero_sums, (regroup(inputs.astype(jnp.float32)), regroup(key_mask), regroup(out_grad)))
    activations = jnp.transpose(states, (1, 0, 2, 3, 4)).reshape(SUBLAYERS, CELLS, LMAX, D)
    stream_grads = jnp.transpose(probe_grads, (1, 0, 2, 3, 4)).reshape(SUBLAYERS, CELLS, LMAX, D)
    return (activations, stream_grads, totals[0], totals[1], totals[2], totals[3], totals[4], totals[5], totals[6], totals[7], totals[8])
```

```python
import math

import jax
import jax.numpy as jnp
from jax import lax
from jax.experimental import pallas as pl
from jax.experimental.pallas import tpu as pltpu
from jax.sharding import PartitionSpec as P

D = 200
HEADS = 10
HEAD_DIM = 64
FEATS = 266
FF = 800
INNER = HEADS * HEAD_DIM
LAYERS = 2
SLOTS = 128
EPSILON = 1e-05

PAIRS = HEADS // 2
MAIN = 256
TAIL = FEATS - MAIN
PAIR_W = 2 * MAIN + 128

LOG2E = math.log2(math.e)
S_FEAT = HEAD_DIM ** (-0.25)
S_NORM = HEAD_DIM ** (-0.5)
Q_SCALE = S_FEAT * LOG2E
SQ_SCALE = 0.5 * S_NORM * LOG2E
SQ_SHIFT = 0.5 * math.log2(FEATS) / HEAD_DIM
MASK_SHIFT = 1000.0
TOTAL_BACK = S_NORM / Q_SCALE

COL = 200
EARLY = [("out", j) for j in range(5)] + [("up", j) for j in range(7)] + [("down", j) for j in range(7)]
D_ROW, E_ROW, C_ROW, A_ROW, B_ROW, G_ROWS = 0, 2048, 3072, 7168, 11264, 14336


def place_columns():
    rows = {}

    def put(l, columns, at):
        for column in columns:
            rows[(l,) + column] = at
            at += COL
        return at

    qkv = [("qkv", j) for j in range(15)]
    ends = [
        put(0, qkv[0:10], D_ROW) + 24,
        put(0, qkv[10:], E_ROW),
        put(0, EARLY, C_ROW),
        put(1, EARLY, A_ROW),
        put(1, qkv, B_ROW) + 24,
    ]
    return rows, ends


ROWS, ENDS = place_columns()
SMALL_ROW = (ENDS[0] - 24, ENDS[4] - 24)

BF = jnp.bfloat16
F32 = jnp.float32


def mm(a, b):
    return jnp.dot(a, b, preferred_element_type=F32)


def mm_t(a, b):
    return lax.dot_general(a, b, (((1,), (1,)), ((), ())), preferred_element_type=F32)


def norm_forward(rows):
    centered = rows - jnp.mean(rows, axis=-1, keepdims=True)
    inverse = lax.rsqrt(jnp.mean(centered * centered, axis=-1, keepdims=True) + EPSILON)
    return centered * inverse, inverse


def build_maps(feats_ref, fw):
    ones = jnp.full((HEAD_DIM, MAIN), -1.0, BF)
    row = lax.broadcasted_iota(jnp.int32, (FEATS, 128), 0)
    lane = lax.broadcasted_iota(jnp.int32, (FEATS, 128), 1)
    tail_lane = lax.broadcasted_iota(jnp.int32, (HEAD_DIM, 128), 1)
    for l in range(LAYERS):
        f = feats_ref[l]
        fw[l, :, 0 : 2 * MAIN] = jnp.zeros((256, 2 * MAIN), BF)
        for hh in range(2):
            pick = jnp.where(row - MAIN == lane - TAIL * hh, 1.0, 0.0)
            pick = jnp.where(row >= MAIN, pick, 0.0).astype(BF)
            tail = mm(f, pick).astype(BF)
            minus = jnp.where(
                (tail_lane >= TAIL * hh) & (tail_lane < TAIL * (hh + 1)), -1.0, 0.0
            ).astype(BF)
            r = HEAD_DIM * hh
            fw[l, r : r + HEAD_DIM, MAIN * hh : MAIN * (hh + 1)] = f[:, 0:MAIN]
            fw[l, 128 + r : 128 + r + HEAD_DIM, MAIN * hh : MAIN * (hh + 1)] = ones
            fw[l, r : r + HEAD_DIM, 2 * MAIN : PAIR_W] = tail
            fw[l, 128 + r : 128 + r + HEAD_DIM, 2 * MAIN : PAIR_W] = minus


def tail_mask():
    row = lax.broadcasted_iota(jnp.int32, (256, 128), 0)
    lane = lax.broadcasted_iota(jnp.int32, (256, 128), 1)
    odd = (row % 128) >= HEAD_DIM
    low = jnp.where(odd, TAIL, 0)
    return jnp.where((lane >= low) & (lane < low + TAIL), 1.0, 0.0)


def store_blocks(target, left, right, mask):
    for hh in range(2):
        r = HEAD_DIM * hh
        lhs = jnp.concatenate(
            [left[r : r + HEAD_DIM], left[128 + r : 128 + r + HEAD_DIM]], axis=0
        )
        block = mm(lhs, right[:, MAIN * hh : MAIN * (hh + 1)]).astype(BF)
        target[r : r + HEAD_DIM, MAIN * hh : MAIN * (hh + 1)] = block[0:HEAD_DIM]
        target[128 + r : 128 + r + HEAD_DIM, MAIN * hh : MAIN * (hh + 1)] = block[HEAD_DIM:]
    target[:, 2 * MAIN : PAIR_W] = (mm(left, right[:, 2 * MAIN : PAIR_W]) * mask).astype(BF)


def pack_columns(g, l, kind, value, columns=None):
    width = value.shape[1]
    columns = range(pl.cdiv(width, 128)) if columns is None else columns
    for n, j in enumerate(columns):
        take = min(128, width - 128 * n)
        at = ROWS[l, kind, j]
        g[at : at + COL, 0:take] = value[:, 128 * n : 128 * n + take]


def pack_row(g, l, row, value):
    width = value.shape[1]
    for j in range(pl.cdiv(width, 128)):
        take = min(128, width - 128 * j)
        at = SMALL_ROW[l] + row + j
        g[at : at + 1, 0:take] = value[:, 128 * j : 128 * j + take]


def clear_gaps(g):
    def clear(start, end):
        if end > start:
            g[start:end, :] = jnp.zeros((end - start, 128), F32)

    for end, limit in zip(ENDS, (E_ROW, C_ROW, A_ROW, B_ROW, G_ROWS)):
        clear(end, limit)
    for l in range(LAYERS):
        clear(SMALL_ROW[l], SMALL_ROW[l] + 24)
        for kind in ("up", "down"):
            clear(ROWS[l, kind, 6], ROWS[l, kind, 6] + COL)


def layers_kernel(
    inputs_hbm,
    lengths,
    gene_mask,
    out_grad_hbm,
    gain,
    bias,
    wqkv_hbm,
    wout_hbm,
    bout,
    feats,
    wup_hbm,
    bup,
    wdown_hbm,
    bdown,
    acts_out,
    sg_out,
    out,
    wqkv,
    wout,
    wup,
    wdown,
    x_in,
    x,
    gr,
    xhat,
    inv,
    normed,
    fw,
    zc,
    vs,
    vt,
    phi,
    kv,
    rden,
    att,
    dn,
    dn_t,
    dqkv,
    hid,
    gp,
    acts,
    sgrads,
    kept,
    g,
    own,
    hop1,
    near1,
    t1,
    near2,
    last,
    relay,
    sems,
    send_sems,
    recv_sems,
    local_sems,
):
    place = Place()
    wire = Wire(send_sems, recv_sems)
    greet(place)
    parts, before = {}, 0
    for name, t, axes, kind in PARTS:
        bufs = (own, hop1, near1, t1, near2, last)
        parts[name] = Part(place, wire, t, axes, kind, before, g, out, bufs)
        before += t
    act_stream = Streams(place, wire, acts, acts_out, relay.at[0])
    sg_stream = Streams(place, wire, sgrads, sg_out, relay.at[1])

    def advance(names):
        for name in names.split():
            if name == "acts":
                act_stream.forward()
            else:
                parts[name].advance()

    section = lax.axis_index("section")
    first = section * 2
    copy_in = pltpu.make_async_copy(inputs_hbm.at[pl.ds(first, 2)], x_in, sems.at[0])
    copy_gr = pltpu.make_async_copy(out_grad_hbm.at[pl.ds(first, 2)], gr, sems.at[1])
    copy_in.start()
    loads = {}
    for l in range(LAYERS):
        for n, (name, src, dst) in enumerate(
            (
                ("qkv", wqkv_hbm, wqkv),
                ("out", wout_hbm, wout),
                ("up", wup_hbm, wup),
                ("down", wdown_hbm, wdown),
            )
        ):
            loads[name, l] = pltpu.make_async_copy(src.at[l], dst.at[l], sems.at[2 + 4 * l + n])
            loads[name, l].start()
    copy_gr.start()
    build_maps(feats, fw)
    mask = tail_mask()
    ones_rows = jnp.ones((128, 128), BF)

    blank = jnp.zeros((LAYERS, 2, PAIRS, HEAD_DIM, MAIN), BF)
    for r in range(4):
        side = MAIN * (1 - r % 2)
        kv[:, :, :, HEAD_DIM * r : HEAD_DIM * (r + 1), side : side + MAIN] = blank
    clear_gaps(g)

    slot = lax.broadcasted_iota(jnp.int32, (128, 128), 1)
    shift = []
    for c in range(2):
        marks = jnp.broadcast_to(gene_mask[pl.ds(first + c, 1), :], (128, 128))
        live = (slot < lengths[first + c]) & (marks > 0)
        shift.append(jnp.where(live, SQ_SHIFT, MASK_SHIFT).T)
    key_shift = jnp.concatenate(shift, axis=0)

    copy_in.wait()
    x[...] = jnp.concatenate([x_in[0].T, x_in[1].T], axis=0).astype(F32)

    def attend_forward(l):
        nx, iv = norm_forward(x[...])
        xhat[l, 0] = nx
        inv[l, 0] = iv
        nb = (nx * gain[l, 0:1] + bias[l, 0:1]).astype(BF)
        normed[l, 0] = nb
        loads["qkv", l].wait()
        for side, shift in ((0, SQ_SHIFT), (1, key_shift)):
            value = mm(nb, wqkv[l, :, INNER * side : INNER * (side + 1)])
            for p in range(PAIRS):
                part = value[:, 128 * p : 128 * (p + 1)]
                zc[l, side, p, :, 0:128] = (part * Q_SCALE).astype(BF)
                zc[l, side, p, :, 128:256] = (part * part * SQ_SCALE + shift).astype(BF)
        v = mm(nb, wqkv[l, :, 2 * INNER : 3 * INNER]).astype(BF)
        vs[l] = v
        vt[...] = v.T

        for side in range(2):
            z = mm(zc[l, side].reshape(PAIRS * 256, 256), fw[l])
            phi[l, side] = jnp.exp2(z).astype(BF).reshape(PAIRS, 256, PAIR_W)
        for p in range(PAIRS):
            for c in range(2):
                rows = slice(128 * c, 128 * (c + 1))
                left = jnp.concatenate([vt[128 * p : 128 * (p + 1), rows], ones_rows], axis=0)
                store_blocks(kv.at[l, c, p], left, phi[l, 1, p, rows], mask)
        for p in range(PAIRS):
            lanes = slice(128 * p, 128 * (p + 1))
            for c in range(2):
                rows = slice(128 * c, 128 * (c + 1))
                nd = mm_t(phi[l, 0, p, rows], kv[l, c, p])
                rd = 1.0 / nd[:, 128:]
                rden[l, rows, lanes] = rd
                att[l, rows, lanes] = (nd[:, 0:128] * rd).astype(BF)
        loads["out", l].wait()
        x[...] = x[...] + mm_t(att[l], wout[l]) + bout[l : l + 1]

    def mix_forward(l):
        nx, iv = norm_forward(x[...])
        xhat[l, 1] = nx
        inv[l, 1] = iv
        nb = (nx * gain[l, 1:2] + bias[l, 1:2]).astype(BF)
        normed[l, 1] = nb
        loads["up", l].wait()
        loads["down", l].wait()
        pre = mm(nb, wup[l]) + bup[l : l + 1]
        cdf = 0.5 * (1.0 + lax.erf(pre * math.sqrt(0.5)))
        hid[l] = (pre * cdf).astype(BF)
        density = jnp.exp(-0.5 * pre * pre) * (1.0 / math.sqrt(2.0 * math.pi))
        gp[l] = (cdf + pre * density).astype(BF)
        x[...] = x[...] + mm_t(hid[l], wdown[l]) + bdown[l : l + 1]

    def norm_backward(l, j, grad_normed):
        nx = xhat[l, j]
        pack_row(g, l, 7 + 2 * j, jnp.sum(grad_normed * nx, axis=0, keepdims=True))
        pack_row(g, l, 11 + 2 * j, jnp.sum(grad_normed, axis=0, keepdims=True))
        scaled = grad_normed * gain[l, j : j + 1]
        return inv[l, j] * (
            scaled
            - jnp.mean(scaled, axis=-1, keepdims=True)
            - nx * jnp.mean(scaled * nx, axis=-1, keepdims=True)
        )

    def mix_backward(l, between):
        low = gr2[...].astype(BF)
        low_t = low.T
        pack_row(g, l, 17, jnp.sum(low.astype(F32), axis=0, keepdims=True))
        pack_columns(g, l, "down", mm(low_t, hid[l]))
        between("mix0")
        dpre = (mm(low, wdown[l]) * gp[l].astype(F32)).astype(BF)
        pack_row(g, l, 0, jnp.sum(dpre.astype(F32), axis=0, keepdims=True))
        between("mix1")
        pack_columns(g, l, "up", mm(normed[l, 1].T, dpre))
        between("mix2")
        gr2[...] = gr2[...] + norm_backward(l, 1, mm_t(dpre, wup[l]))
        between("mix3")

    def attend_backward(l, between):
        low = gr2[...].astype(BF)
        low_t = low.T
        pack_row(g, l, 15, jnp.sum(low.astype(F32), axis=0, keepdims=True))
        pack_columns(g, l, "out", mm(low_t, att[l]))
        datt = mm(low, wout[l])
        dnum = datt * rden[l]
        dden = -dnum * att[l].astype(F32)
        for p in range(PAIRS):
            lanes = slice(128 * p, 128 * (p + 1))
            dn[p, :, 0:128] = dnum[:, lanes].astype(BF)
            dn[p, :, 128:256] = dden[:, lanes].astype(BF)
            dn_t[p] = dn[p].T
        normed_t = normed[l, 0].T
        between("pre")
        for p in range(PAIRS):
            for c in range(2):
                rows = slice(128 * c, 128 * (c + 1))
                phi_q = phi[l, 0, p, rows]
                dzq = mm(dn[p, rows], kv[l, c, p]).astype(BF) * phi_q
                store_blocks(kv.at[l, c, p], dn_t[p, :, rows], phi_q, mask)
                phi[l, 0, p, rows] = dzq
            between(f"q{p}")
        for p in range(PAIRS):
            lanes = slice(128 * p, 128 * (p + 1))
            for c in range(2):
                rows = slice(128 * c, 128 * (c + 1))
                phi_k = phi[l, 1, p, rows]
                vh = jnp.concatenate([vs[l, rows, lanes], ones_rows], axis=1)
                dzk = mm(vh, kv[l, c, p]).astype(BF) * phi_k
                dv = mm_t(phi_k, kv[l, c, p, 0:128])
                dqkv[rows, 2 * INNER + 128 * p : 2 * INNER + 128 * (p + 1)] = dv.astype(BF)
                phi[l, 1, p, rows] = dzk
            if p == PAIRS - 1:
                pack_columns(g, l, "qkv", mm(normed_t, dqkv[:, 2 * INNER :]), range(10, 15))
            between(f"k{p}")

        for side in range(2):
            b = mm_t(phi[l, side].reshape(PAIRS * 256, PAIR_W), fw[l]).reshape(PAIRS, 256, 256)
            for p in range(PAIRS):
                own = zc[l, side, p, :, 0:128].astype(F32) * TOTAL_BACK
                value = b[p, :, 0:128] * S_FEAT + b[p, :, 128:256] * own
                at = INNER * side + 128 * p
                dqkv[:, at : at + 128] = value.astype(BF)
        between("back")
        pack_columns(g, l, "qkv", mm(normed_t, dqkv[:, 0 : 2 * INNER]), range(10))
        gr2[...] = gr2[...] + norm_backward(l, 0, mm_t(dqkv[...], wqkv[l]))
        between("post")

    gr2 = x

    def turn_stream(target, s, value):
        for c in range(2):
            target[s, c] = value[SLOTS * c : SLOTS * (c + 1)].T

    for l in range(LAYERS):
        attend_forward(l)
        turn_stream(acts, 2 * l, x[...])
        mix_forward(l)
        turn_stream(acts, 2 * l + 1, x[...])
    copy_gr.wait()
    gr2[...] = jnp.concatenate([gr[0].T, gr[1].T], axis=0)
    await_greetings(10)
    act_stream.start(local_sems.at[0])
    for l in reversed(range(LAYERS)):
        mix_backward(l, lambda at: advance(DURING[l].get(at, "")))
        kept[2 * l + 1] = gr2[...]
        attend_backward(l, lambda at: advance(DURING[l].get(at, "")))
        kept[2 * l] = gr2[...]
    for n, name in enumerate(BEHIND):
        if name == "sg":
            sg_stream.forward()
        else:
            parts[name].advance()
        if n == 2:
            for turn in range(2 * LAYERS):
                turn_stream(sgrads, turn, kept[turn])
            sg_stream.start(local_sems.at[1])
            act_stream.finish()
        wire.drain(max(len(wire.sent) - 72, 0))
    sg_stream.finish()
    wire.drain(len(wire.sent))


def layers(args):
    vmem = pl.BlockSpec(memory_space=pltpu.VMEM)
    hbm = pl.BlockSpec(memory_space=pl.ANY)
    smem = pl.BlockSpec(memory_space=pltpu.SMEM)
    rows = 2 * SLOTS

    def shape(*dims):
        return jax.ShapeDtypeStruct(dims, F32)

    def share(n, *lead):
        return pltpu.VMEM(lead + (n * SHARE, 128), F32)

    scratch = [
        pltpu.VMEM((LAYERS, D, 3 * INNER), BF),
        pltpu.VMEM((LAYERS, D, INNER), BF),
        pltpu.VMEM((LAYERS, D, FF), BF),
        pltpu.VMEM((LAYERS, D, FF), BF),
        pltpu.VMEM((2, D, SLOTS), BF),
        pltpu.VMEM((rows, D), F32),
        pltpu.VMEM((2, D, SLOTS), F32),
        pltpu.VMEM((LAYERS, 2, rows, D), F32),
        pltpu.VMEM((LAYERS, 2, rows, 1), F32),
        pltpu.VMEM((LAYERS, 2, rows, D), BF),
        pltpu.VMEM((LAYERS, 256, PAIR_W), BF),
        pltpu.VMEM((LAYERS, 2, PAIRS, rows, 256), BF),
        pltpu.VMEM((LAYERS, rows, INNER), BF),
        pltpu.VMEM((INNER, rows), BF),
        pltpu.VMEM((LAYERS, 2, PAIRS, rows, PAIR_W), BF),
        pltpu.VMEM((LAYERS, 2, PAIRS, 256, PAIR_W), BF),
        pltpu.VMEM((LAYERS, rows, INNER), F32),
        pltpu.VMEM((LAYERS, rows, INNER), BF),
        pltpu.VMEM((PAIRS, rows, 256), BF),
        pltpu.VMEM((PAIRS, 256, rows), BF),
        pltpu.VMEM((rows, 3 * INNER), BF),
        pltpu.VMEM((LAYERS, rows, FF), BF),
        pltpu.VMEM((LAYERS, rows, FF), BF),
        pltpu.VMEM((2 * LAYERS, 2, D, SLOTS), F32),
        pltpu.VMEM((2 * LAYERS, 2, D, SLOTS), F32),
        pltpu.VMEM((2 * LAYERS, rows, D), F32),
        share(1024),
        share(512),
        share(128),
        share(128, 3),
        share(128),
        share(32, 3),
        share(32, 4),
        pltpu.VMEM((2, 2, D, SLOTS), F32),
        pltpu.SemaphoreType.DMA((2 + 4 * LAYERS,)),
        pltpu.SemaphoreType.DMA((SENDS,)),
        pltpu.SemaphoreType.DMA((SENDS,)),
        pltpu.SemaphoreType.DMA((2,)),
    ]
    return pl.pallas_call(
        layers_kernel,
        out_shape=(
            pltpu.VMEM((8, D, SLOTS), F32),
            pltpu.VMEM((8, D, SLOTS), F32),
            pltpu.VMEM((1024 * SHARE, 128), F32),
        ),
        in_specs=[hbm, smem, vmem, hbm, vmem, vmem, hbm, hbm, vmem, vmem, hbm, vmem, hbm, vmem],
        out_specs=(vmem, vmem, vmem),
        scratch_shapes=scratch,
        compiler_params=pltpu.CompilerParams(
            vmem_limit_bytes=53 * 1024 * 1024, collective_id=0, has_side_effects=True
        ),
        name="layers",
    )(*args)


MESH = pl.DeviceIdType.MESH

PARTS = (
    ("D0", 1, "yzx", False),
    ("D1", 1, "zxy", False),
    ("E0", 1, "yxz", True),
    ("C0", 3, "xyz", True),
    ("C1", 1, "zxy", True),
    ("A0", 4, "zyx", True),
    ("B0", 3, "yxz", True),
)
SHARE = sum(part[1] for part in PARTS)
SENDS = 20 * len(PARTS) + 12

DURING = (
    {"pre": "C0 B0 C1", "k0": "A0", "k4": "E0", "back": "C0 C1 B0", "post": "D1 E0 D0"},
    {"pre": "A0", "k0": "acts", "post": "B0 A0"},
)
BEHIND = (
    "A0", "C1", "D1", "C0", "D0", "B0", "E0", "A0",
    "C0", "B0", "C1", "D0", "E0", "sg", "D1", "C0",
    "A0", "C1", "E0", "D1", "B0", "D0", "A0", "C0",
    "C1", "E0", "D1", "B0", "D0", "A0", "C0", "C1",
    "E0", "D1", "B0", "D0", "C0", "E0", "A0", "C1",
    "B0", "C0", "A0", "D1", "C1", "D0", "B0", "E0",
    "C0", "D1", "C1", "D0", "E0",
)


class Place:
    def __init__(self):
        self.dp = lax.axis_index("dp")
        self.section = lax.axis_index("section")
        self.core = lax.rem(self.dp, 2)
        self.at = {
            "x": lax.rem(self.dp // 2, 4),
            "y": self.dp // 8,
            "z": self.section,
        }

        self.ahead, self.behind = 1 + 2 * self.core, 3 - 2 * self.core
        self.steps, self.peers = {}, {}

    def step(self, axis, by):
        key = axis, by if isinstance(by, int) else id(by)
        if key not in self.steps:
            self.steps[key] = lax.rem(self.at[axis] + by, 4)
        return self.steps[key]

    def peer(self, axis, by):
        key = axis, by if isinstance(by, int) else id(by)
        if key not in self.peers:
            self.peers[key] = self.find_peer(axis, by)
        return self.peers[key]

    def find_peer(self, axis, by):
        if axis == "core":
            return {"dp": self.dp + 1 - 2 * self.core, "section": self.section}
        to = self.step(axis, by)
        if axis == "z":
            return {"dp": self.dp, "section": to}
        stride = 2 if axis == "x" else 8
        return {"dp": self.dp + stride * (to - self.at[axis]), "section": self.section}


class Wire:
    def __init__(self, send_sems, recv_sems):
        self.send_sems, self.recv_sems = send_sems, recv_sems
        self.sent = []
        self.drained = 0

    def send(self, src, dst, to):
        n = len(self.sent)
        copy = pltpu.make_async_remote_copy(
            src_ref=src,
            dst_ref=dst,
            send_sem=self.send_sems.at[n],
            recv_sem=self.recv_sems.at[n],
            device_id=to,
            device_id_type=MESH,
        )
        copy.start()
        self.sent.append(copy)
        return copy

    def drain(self, end):
        for copy in self.sent[self.drained : end]:
            copy.wait_send()
        self.drained = end


def greet(place):
    barrier = pltpu.get_barrier_semaphore()
    peers = [place.peer("core", 1)]
    peers += [place.peer(axis, by) for axis in "xyz" for by in (1, 2, 3)]
    for peer in peers:
        pl.semaphore_signal(barrier, inc=1, device_id=peer, device_id_type=MESH)


def await_greetings(count):
    pl.semaphore_wait(pltpu.get_barrier_semaphore(), count)


class Streams:
    def __init__(self, place, wire, source, target, relay):
        self.place, self.wire, self.source, self.target, self.relay = (
            place,
            wire,
            source,
            target,
            relay,
        )

    def start(self, local_sem):
        p, w = self.place, self.wire
        me, right, left, far = (p.step("z", by) for by in (0, 1, 3, 2))
        self.hops = [
            w.send(self.source.at[far, 0], self.relay.at[0], p.peer("z", 1)),
            w.send(self.source.at[far, 1], self.relay.at[1], p.peer("z", 3)),
        ]
        own = self.target.at[pl.ds(2 * me, 2)]
        self.direct = [
            w.send(self.source.at[right], own, p.peer("z", 1)),
            w.send(self.source.at[left], own, p.peer("z", 3)),
        ]
        self.local = pltpu.make_async_copy(self.source.at[me], own, local_sem)
        self.local.start()

    def forward(self):
        p, w = self.place, self.wire
        self.hops[0].wait_recv()
        self.direct.append(
            w.send(self.relay.at[0], self.target.at[2 * p.step("z", 3)], p.peer("z", 1))
        )
        self.hops[1].wait_recv()
        self.direct.append(
            w.send(self.relay.at[1], self.target.at[2 * p.step("z", 1) + 1], p.peer("z", 3))
        )

    def finish(self):
        for copy in self.direct:
            copy.wait_recv()
        self.local.wait()


class Quarters:
    def __init__(self, place, wire, axis, quarter):
        self.place, self.wire, self.axis, self.quarter = place, wire, axis, quarter

    def rows(self, by, base=0):
        start = base + self.place.step(self.axis, by) * self.quarter
        return pl.ds(pl.multiple_of(start, 8), self.quarter)

    def begin(self, block, near):
        self.block, self.near, self.got = block, near, []

    def send(self, by):
        src, dst = self.block.at[self.rows(by)], self.near.at[by - 1]
        self.got.append(self.wire.send(src, dst, self.place.peer(self.axis, by)))

    def result(self, block):
        for copy in self.got:
            copy.wait_recv()
        return (block[self.rows(0), :] + self.near[0]) + (self.near[1] + self.near[2])

    def spread(self, out, base):
        view = out.at[self.rows(0, base)]
        self.back = [
            self.wire.send(view, view, self.place.peer(self.axis, by)) for by in (2, 1, 3)
        ]

    def arrivals(self):
        return zip(self.back, (2, 3, 1))

    def spread_end(self):
        for copy in self.back:
            copy.wait_recv()


class Ring:
    def __init__(self, place, wire, axis, quarter):
        self.place, self.wire, self.axis, self.quarter = place, wire, axis, quarter
        self.ahead, self.behind = place.ahead, place.behind
        self.to_ahead = place.peer(axis, self.ahead)
        self.to_behind = place.peer(axis, self.behind)

    def buffers(self, hop, near):
        self.hop, self.near = hop, near

    def rows(self, by, base=0):
        start = base + self.place.step(self.axis, by) * self.quarter
        return pl.ds(pl.multiple_of(start, 8), self.quarter)

    def send_far(self, block):
        self.far = self.wire.send(block.at[self.rows(2)], self.hop, self.to_ahead)

    def send_near(self, block):
        src = block.at[self.rows(self.behind)]
        self.got = [self.wire.send(src, self.near.at[1], self.to_behind)]

    def send_sum(self, block):
        self.far.wait_recv()
        self.hop[...] = self.hop[...] + block[self.rows(self.ahead), :]
        self.got.append(self.wire.send(self.hop, self.near.at[0], self.to_ahead))

    def result(self, block):
        for copy in self.got:
            copy.wait_recv()
        return block[self.rows(0), :] + self.near[0] + self.near[1]

    def spread(self, out, base):
        w = self.wire
        view = out.at[self.rows(0, base)]
        self.first = w.send(view, view, self.to_ahead)
        self.others = [w.send(view, view, self.to_behind)]

    def spread_on(self, out, base):
        self.first.wait_recv()
        view = out.at[self.rows(self.behind, base)]
        self.others.append(self.wire.send(view, view, self.to_ahead))

    def arrivals(self):
        return zip(self.others, (self.ahead, 2))


class Part:
    def __init__(self, place, wire, tiles, axes, ring, before, g, out, bufs):
        self.place, self.wire, self.axes, self.g, self.out = place, wire, axes, g, out
        t, b = tiles, before
        self.t, self.b = t, b
        base, core = 1024 * b, place.core
        self.mine = pl.multiple_of(base + core * (512 * t), 8)
        self.other = pl.multiple_of(base + (1 - core) * (512 * t), 8)
        self.at1 = self.mine + place.at[axes[0]] * (128 * t)
        self.at2 = self.at1 + place.at[axes[1]] * (32 * t)
        own, hop1, near1, t1, near2, last = bufs
        self.own_all = own
        self.own = own.at[self.spot(512)]
        self.near1 = near1.at[:, self.spot(128)]
        self.t1 = t1.at[self.spot(128)]
        self.near2 = near2.at[:, self.spot(32)]
        self.last = last.at[:, self.spot(32)]
        self.phase2 = Quarters(place, wire, axes[1], 32 * t)
        self.at = 0
        if ring:
            self.phase1 = Ring(place, wire, axes[0], 128 * t)
            self.phase1.buffers(hop1.at[self.spot(128)], self.near1)
            self.steps = [
                self.swap,
                self.join_ring,
                self.sums,
                self.second,
                self.third,
                self.total,
                self.back1,
                self.back1_on,
                self.give_rest,
                self.taken,
            ]
        else:
            self.phase1 = Quarters(place, wire, axes[0], 128 * t)
            self.steps = [
                self.swap,
                self.join,
                self.second,
                self.third,
                self.total,
                self.back1,
                self.give_rest,
                self.taken,
            ]

    def advance(self):
        self.steps[self.at]()
        self.at += 1

    def spot(self, rows):
        return pl.ds(rows * self.b, rows * self.t)

    def swap(self):
        src = self.g.at[pl.ds(self.other, 512 * self.t)]
        self.swapped = self.wire.send(src, self.own, self.place.peer("core", 1))

    def add_quarter(self, by):
        rows = 128 * self.t
        start = self.place.step(self.axes[0], by) * rows
        to = pl.ds(pl.multiple_of(512 * self.b + start, 8), rows)
        mine = pl.ds(pl.multiple_of(self.mine + start, 8), rows)
        self.own_all[to, :] = self.own_all[to, :] + self.g[mine, :]

    def join(self):
        self.swapped.wait_recv()
        self.phase1.begin(self.own, self.near1)
        for by in (2, 1, 3):
            self.add_quarter(by)
            self.phase1.send(by)
        self.add_quarter(0)

    def join_ring(self):
        self.swapped.wait_recv()
        self.add_quarter(2)
        self.phase1.send_far(self.own)
        self.add_quarter(self.place.behind)
        self.phase1.send_near(self.own)
        self.add_quarter(self.place.ahead)
        self.add_quarter(0)

    def sums(self):
        self.phase1.send_sum(self.own)

    def second(self):
        self.t1[...] = self.phase1.result(self.own)
        self.phase2.begin(self.t1, self.near2)
        for by in (2, 1, 3):
            self.phase2.send(by)

    def third(self):
        here = self.place.at[self.axes[2]]
        self.last[here] = self.phase2.result(self.t1)
        view = self.last.at[here]
        self.thirds = [
            self.wire.send(view, view, self.place.peer(self.axes[2], by)) for by in (2, 1, 3)
        ]

    def total(self):
        for copy in self.thirds:
            copy.wait_recv()
        z = self.last
        rows = pl.ds(pl.multiple_of(self.at2, 8), 32 * self.t)
        self.out[rows, :] = (z[0] + z[1]) + (z[2] + z[3])
        self.phase2.spread(self.out, self.at1)

    def back1(self):
        self.phase2.spread_end()
        self.phase1.spread(self.out, self.mine)
        self.given = []
        self.give(0)

    def back1_on(self):
        self.phase1.spread_on(self.out, self.mine)
        self.give(self.place.behind)

    def give(self, by):
        view = self.out.at[self.phase1.rows(by, self.mine)]
        self.given.append(self.wire.send(view, view, self.place.peer("core", 1)))

    def give_rest(self):
        for copy, by in self.phase1.arrivals():
            copy.wait_recv()
            self.give(by)

    def taken(self):
        for copy in self.given:
            copy.wait_recv()


def finish_kernel(
    acts,
    sgrads,
    out,
    acts_out,
    sg_out,
    gains,
    shifts,
    qkv_out,
    out_out,
    bout,
    up_out,
    bup,
    down_out,
    bdown,
    qkv,
    out_w,
    up,
    down,
    sems,
):
    copies = []

    def start(src, dst):
        copies.append(pltpu.make_async_copy(src, dst, sems.at[len(copies)]))
        copies[-1].start()

    start(acts, acts_out)
    start(sgrads, sg_out)
    for l in range(LAYERS):
        for kind, target, result, width in (
            ("qkv", qkv, qkv_out, 3 * INNER),
            ("out", out_w, out_out, INNER),
            ("up", up, up_out, FF),
            ("down", down, down_out, FF),
        ):
            for j in range(pl.cdiv(width, 128)):
                take = min(128, width - 128 * j)
                at = ROWS[l, kind, j]
                target[l, :, 128 * j : 128 * j + take] = out[at : at + COL, 0:take]
            start(target.at[l], result.at[l])
    write_small(out, gains, shifts, bout, bup, bdown)
    for copy in copies:
        copy.wait()


def finish(acts, sgrads, out):
    vmem = pl.BlockSpec(memory_space=pltpu.VMEM)
    hbm = pl.BlockSpec(memory_space=pl.ANY)

    def shape(*dims):
        return jax.ShapeDtypeStruct(dims, F32)

    return pl.pallas_call(
        finish_kernel,
        out_shape=(
            shape(8, D, SLOTS),
            shape(8, D, SLOTS),
            shape(LAYERS, 2, D),
            shape(LAYERS, 2, D),
            shape(LAYERS, D, 3 * INNER),
            shape(LAYERS, D, INNER),
            shape(LAYERS, D),
            shape(LAYERS, D, FF),
            shape(LAYERS, FF),
            shape(LAYERS, D, FF),
            shape(LAYERS, D),
        ),
        in_specs=[vmem, vmem, vmem],
        out_specs=(hbm, hbm, vmem, vmem, hbm, hbm, vmem, hbm, vmem, hbm, vmem),
        scratch_shapes=[
            pltpu.VMEM((LAYERS, D, 3 * INNER), F32),
            pltpu.VMEM((LAYERS, D, INNER), F32),
            pltpu.VMEM((LAYERS, D, FF), F32),
            pltpu.VMEM((LAYERS, D, FF), F32),
            pltpu.SemaphoreType.DMA((2 + 4 * LAYERS,)),
        ],
        compiler_params=pltpu.CompilerParams(vmem_limit_bytes=24 * 1024 * 1024),
        name="finish",
    )(acts, sgrads, out)


def write_small(out, gains, shifts, bout, bup, bdown):
    for l in range(LAYERS):

        def row(at, width):
            start = SMALL_ROW[l] + at
            rows = [out[start + j : start + j + 1, :] for j in range(pl.cdiv(width, 128))]
            return jnp.concatenate(rows, axis=1)[:, 0:width]

        for j in range(2):
            gains[l, j : j + 1, :] = row(7 + 2 * j, D)
            shifts[l, j : j + 1, :] = row(11 + 2 * j, D)
        bout[l : l + 1, :] = row(15, D)
        bup[l : l + 1, :] = row(0, FF)
        bdown[l : l + 1, :] = row(17, D)


def body(
    inputs,
    lengths,
    gene_mask,
    out_grad,
    gain,
    bias,
    wqkv,
    wout,
    bout,
    feats,
    wup,
    bup,
    wdown,
    bdown,
):
    def flip(value):
        return jnp.swapaxes(value, -1, -2)

    streams_and_sums = layers(
        (
            flip(inputs),
            lengths,
            gene_mask,
            flip(out_grad),
            gain,
            bias,
            wqkv,
            flip(wout),
            bout,
            feats,
            wup,
            bup,
            flip(wdown),
            bdown,
        )
    )
    acts, sgrads, gains, shifts, qkv, out, dbout, up, dbup, down, dbdown = finish(*streams_and_sums)
    return (
        flip(acts)[None],
        flip(sgrads)[None],
        gains,
        shifts,
        qkv,
        flip(out),
        dbout,
        up,
        dbup,
        flip(down),
        dbdown,
    )


def solution(mesh):
    placed = (
        P("dp", None, None),
        P("dp"),
        P("dp", None),
        P("dp", None, None),
    ) + (P(),) * 10
    return jax.shard_map(
        body,
        mesh=mesh,
        in_specs=placed,
        out_specs=(P("section", "dp", None, None),) * 2 + (P(),) * 9,
        check_vma=False,
    )
```

```python
import math

import jax
import jax.numpy as jnp
from jax import lax
from jax.experimental import pallas as pl
from jax.experimental.pallas import tpu as pltpu
from jax.sharding import PartitionSpec as P

D = 200
HEADS = 10
HEAD_DIM = 64
FEATS = 266
FF = 800
INNER = HEADS * HEAD_DIM
LAYERS = 2
SLOTS = 128
EPSILON = 1e-05

PAIRS = HEADS // 2
MAIN = 256
TAIL = FEATS - MAIN
PAIR_W = 2 * MAIN + 128

LOG2E = math.log2(math.e)
S_FEAT = HEAD_DIM ** (-0.25)
S_NORM = HEAD_DIM ** (-0.5)
Q_SCALE = S_FEAT * LOG2E
SQ_SCALE = 0.5 * S_NORM * LOG2E
SQ_SHIFT = 0.5 * math.log2(FEATS) / HEAD_DIM
MASK_SHIFT = 1000.0
TOTAL_BACK = S_NORM / Q_SCALE

COL = 200
QK = [("qkv", j) for j in range(10)]
OUT_V = [("out", j) for j in range(5)] + [("qkv", j) for j in range(10, 15)]
UP_DOWN = [("up", j) for j in range(7)] + [("down", j) for j in range(7)]
D_ROW, E_ROW, C_ROW, A_ROW, F_ROW, B_ROW, G_ROWS = 0, 2048, 4096, 6912, 9728, 11776, 13824


def place_columns():
    rows = {}

    def put(l, columns, at):
        for column in columns:
            rows[(l,) + column] = at
            at += COL
        return at

    ends = [
        put(0, QK, D_ROW) + 24,
        put(0, OUT_V, E_ROW),
        put(0, UP_DOWN, C_ROW),
        put(1, UP_DOWN, A_ROW),
        put(1, OUT_V, F_ROW),
        put(1, QK, B_ROW) + 24,
    ]
    return rows, ends


ROWS, ENDS = place_columns()
SMALL_ROW = (ENDS[0] - 24, ENDS[5] - 24)

BF = jnp.bfloat16
F32 = jnp.float32


def mm(a, b):
    return jnp.dot(a, b, preferred_element_type=F32)


def mm_t(a, b):
    return lax.dot_general(a, b, (((1,), (1,)), ((), ())), preferred_element_type=F32)


def norm_forward(rows):
    centered = rows - jnp.mean(rows, axis=-1, keepdims=True)
    inverse = lax.rsqrt(jnp.mean(centered * centered, axis=-1, keepdims=True) + EPSILON)
    return centered * inverse, inverse


def build_maps(feats_ref, fw):
    ones = jnp.full((HEAD_DIM, MAIN), -1.0, BF)
    row = lax.broadcasted_iota(jnp.int32, (FEATS, 128), 0)
    lane = lax.broadcasted_iota(jnp.int32, (FEATS, 128), 1)
    tail_lane = lax.broadcasted_iota(jnp.int32, (HEAD_DIM, 128), 1)
    for l in range(LAYERS):
        f = feats_ref[l]
        fw[l, :, 0 : 2 * MAIN] = jnp.zeros((256, 2 * MAIN), BF)
        for hh in range(2):
            pick = jnp.where(row - MAIN == lane - TAIL * hh, 1.0, 0.0)
            pick = jnp.where(row >= MAIN, pick, 0.0).astype(BF)
            tail = mm(f, pick).astype(BF)
            minus = jnp.where(
                (tail_lane >= TAIL * hh) & (tail_lane < TAIL * (hh + 1)), -1.0, 0.0
            ).astype(BF)
            r = HEAD_DIM * hh
            fw[l, r : r + HEAD_DIM, MAIN * hh : MAIN * (hh + 1)] = f[:, 0:MAIN]
            fw[l, 128 + r : 128 + r + HEAD_DIM, MAIN * hh : MAIN * (hh + 1)] = ones
            fw[l, r : r + HEAD_DIM, 2 * MAIN : PAIR_W] = tail
            fw[l, 128 + r : 128 + r + HEAD_DIM, 2 * MAIN : PAIR_W] = minus


def tail_mask():
    row = lax.broadcasted_iota(jnp.int32, (256, 128), 0)
    lane = lax.broadcasted_iota(jnp.int32, (256, 128), 1)
    odd = (row % 128) >= HEAD_DIM
    low = jnp.where(odd, TAIL, 0)
    return jnp.where((lane >= low) & (lane < low + TAIL), 1.0, 0.0)


def store_blocks(target, left, right, mask):
    for hh in range(2):
        r = HEAD_DIM * hh
        lhs = jnp.concatenate(
            [left[r : r + HEAD_DIM], left[128 + r : 128 + r + HEAD_DIM]], axis=0
        )
        block = mm(lhs, right[:, MAIN * hh : MAIN * (hh + 1)]).astype(BF)
        target[r : r + HEAD_DIM, MAIN * hh : MAIN * (hh + 1)] = block[0:HEAD_DIM]
        target[128 + r : 128 + r + HEAD_DIM, MAIN * hh : MAIN * (hh + 1)] = block[HEAD_DIM:]
    target[:, 2 * MAIN : PAIR_W] = (mm(left, right[:, 2 * MAIN : PAIR_W]) * mask).astype(BF)


def pack_columns(g, l, kind, value, columns=None):
    width = value.shape[1]
    columns = range(pl.cdiv(width, 128)) if columns is None else columns
    for n, j in enumerate(columns):
        take = min(128, width - 128 * n)
        at = ROWS[l, kind, j]
        g[at : at + COL, 0:take] = value[:, 128 * n : 128 * n + take]


def pack_row(g, l, row, value):
    width = value.shape[1]
    for j in range(pl.cdiv(width, 128)):
        take = min(128, width - 128 * j)
        at = SMALL_ROW[l] + row + j
        g[at : at + 1, 0:take] = value[:, 128 * j : 128 * j + take]


def clear_gaps(g):
    def clear(start, end):
        if end > start:
            g[start:end, :] = jnp.zeros((end - start, 128), F32)

    for end, limit in zip(ENDS, (E_ROW, C_ROW, A_ROW, F_ROW, B_ROW, G_ROWS)):
        clear(end, limit)
    for l in range(LAYERS):
        clear(SMALL_ROW[l], SMALL_ROW[l] + 24)
        for kind in ("up", "down"):
            clear(ROWS[l, kind, 6], ROWS[l, kind, 6] + COL)


def layers_kernel(
    inputs_hbm,
    lengths,
    gene_mask,
    out_grad_hbm,
    gain,
    bias,
    wqkv_hbm,
    wout_hbm,
    bout,
    feats,
    wup_hbm,
    bup,
    wdown_hbm,
    bdown,
    acts_out,
    sg_out,
    out,
    wqkv,
    wout,
    wup,
    wdown,
    x_in,
    x,
    gr,
    xhat,
    inv,
    normed,
    fw,
    zc,
    vs,
    vt,
    phi,
    kv,
    rden,
    att,
    dn,
    dn_t,
    dqkv,
    hid,
    gp,
    acts,
    sgrads,
    kept,
    g,
    own,
    hop1,
    near1,
    t1,
    hop2,
    near2,
    last,
    relay,
    sems,
    send_sems,
    recv_sems,
    local_sems,
):
    place = Place()
    wire = Wire(send_sems, recv_sems)
    greet(place)
    parts, before = {}, 0
    for name, t, axes, kind in PARTS:
        bufs = (own, hop1, near1, t1, hop2, near2, last)
        parts[name] = Part(place, wire, t, axes, kind, before, g, out, bufs)
        before += t
    act_stream = Streams(place, wire, acts, acts_out, relay.at[0])
    sg_stream = Streams(place, wire, sgrads, sg_out, relay.at[1])

    def advance(names):
        for name in names.split():
            if name == "acts":
                act_stream.forward()
            else:
                parts[name].advance()

    section = lax.axis_index("section")
    first = section * 2
    copy_in = pltpu.make_async_copy(inputs_hbm.at[pl.ds(first, 2)], x_in, sems.at[0])
    copy_gr = pltpu.make_async_copy(out_grad_hbm.at[pl.ds(first, 2)], gr, sems.at[1])
    copy_in.start()
    loads = {}
    for l in range(LAYERS):
        for n, (name, src, dst) in enumerate(
            (
                ("qkv", wqkv_hbm, wqkv),
                ("out", wout_hbm, wout),
                ("up", wup_hbm, wup),
                ("down", wdown_hbm, wdown),
            )
        ):
            loads[name, l] = pltpu.make_async_copy(src.at[l], dst.at[l], sems.at[2 + 4 * l + n])
            loads[name, l].start()
    copy_gr.start()
    build_maps(feats, fw)
    mask = tail_mask()
    ones_rows = jnp.ones((128, 128), BF)

    blank = jnp.zeros((LAYERS, 2, PAIRS, HEAD_DIM, MAIN), BF)
    for r in range(4):
        side = MAIN * (1 - r % 2)
        kv[:, :, :, HEAD_DIM * r : HEAD_DIM * (r + 1), side : side + MAIN] = blank
    clear_gaps(g)

    slot = lax.broadcasted_iota(jnp.int32, (128, 128), 1)
    shift = []
    for c in range(2):
        marks = jnp.broadcast_to(gene_mask[pl.ds(first + c, 1), :], (128, 128))
        live = (slot < lengths[first + c]) & (marks > 0)
        shift.append(jnp.where(live, SQ_SHIFT, MASK_SHIFT).T)
    key_shift = jnp.concatenate(shift, axis=0)

    copy_in.wait()
    x[...] = jnp.concatenate([x_in[0].T, x_in[1].T], axis=0).astype(F32)

    def attend_forward(l):
        nx, iv = norm_forward(x[...])
        xhat[l, 0] = nx
        inv[l, 0] = iv
        nb = (nx * gain[l, 0:1] + bias[l, 0:1]).astype(BF)
        normed[l, 0] = nb
        loads["qkv", l].wait()
        for side, shift in ((0, SQ_SHIFT), (1, key_shift)):
            value = mm(nb, wqkv[l, :, INNER * side : INNER * (side + 1)])
            for p in range(PAIRS):
                part = value[:, 128 * p : 128 * (p + 1)]
                zc[l, side, p, :, 0:128] = (part * Q_SCALE).astype(BF)
                zc[l, side, p, :, 128:256] = (part * part * SQ_SCALE + shift).astype(BF)
        v = mm(nb, wqkv[l, :, 2 * INNER : 3 * INNER]).astype(BF)
        vs[l] = v
        vt[...] = v.T

        for side in range(2):
            z = mm(zc[l, side].reshape(PAIRS * 256, 256), fw[l])
            phi[l, side] = jnp.exp2(z).astype(BF).reshape(PAIRS, 256, PAIR_W)
        for p in range(PAIRS):
            for c in range(2):
                rows = slice(128 * c, 128 * (c + 1))
                left = jnp.concatenate([vt[128 * p : 128 * (p + 1), rows], ones_rows], axis=0)
                store_blocks(kv.at[l, c, p], left, phi[l, 1, p, rows], mask)
        for p in range(PAIRS):
            lanes = slice(128 * p, 128 * (p + 1))
            for c in range(2):
                rows = slice(128 * c, 128 * (c + 1))
                nd = mm_t(phi[l, 0, p, rows], kv[l, c, p])
                rd = 1.0 / nd[:, 128:]
                rden[l, rows, lanes] = rd
                att[l, rows, lanes] = (nd[:, 0:128] * rd).astype(BF)
        loads["out", l].wait()
        x[...] = x[...] + mm_t(att[l], wout[l]) + bout[l : l + 1]

    def mix_forward(l):
        nx, iv = norm_forward(x[...])
        xhat[l, 1] = nx
        inv[l, 1] = iv
        nb = (nx * gain[l, 1:2] + bias[l, 1:2]).astype(BF)
        normed[l, 1] = nb
        loads["up", l].wait()
        loads["down", l].wait()
        pre = mm(nb, wup[l]) + bup[l : l + 1]
        cdf = 0.5 * (1.0 + lax.erf(pre * math.sqrt(0.5)))
        hid[l] = (pre * cdf).astype(BF)
        density = jnp.exp(-0.5 * pre * pre) * (1.0 / math.sqrt(2.0 * math.pi))
        gp[l] = (cdf + pre * density).astype(BF)
        x[...] = x[...] + mm_t(hid[l], wdown[l]) + bdown[l : l + 1]

    def norm_backward(l, j, grad_normed):
        nx = xhat[l, j]
        pack_row(g, l, 7 + 2 * j, jnp.sum(grad_normed * nx, axis=0, keepdims=True))
        pack_row(g, l, 11 + 2 * j, jnp.sum(grad_normed, axis=0, keepdims=True))
        scaled = grad_normed * gain[l, j : j + 1]
        return inv[l, j] * (
            scaled
            - jnp.mean(scaled, axis=-1, keepdims=True)
            - nx * jnp.mean(scaled * nx, axis=-1, keepdims=True)
        )

    def mix_backward(l, between):
        low = gr2[...].astype(BF)
        low_t = low.T
        pack_row(g, l, 17, jnp.sum(low.astype(F32), axis=0, keepdims=True))
        pack_columns(g, l, "down", mm(low_t, hid[l]))
        between("mix0")
        dpre = (mm(low, wdown[l]) * gp[l].astype(F32)).astype(BF)
        pack_row(g, l, 0, jnp.sum(dpre.astype(F32), axis=0, keepdims=True))
        between("mix1")
        pack_columns(g, l, "up", mm(normed[l, 1].T, dpre))
        between("mix2")
        gr2[...] = gr2[...] + norm_backward(l, 1, mm_t(dpre, wup[l]))
        between("mix3")

    def attend_backward(l, between):
        low = gr2[...].astype(BF)
        low_t = low.T
        pack_row(g, l, 15, jnp.sum(low.astype(F32), axis=0, keepdims=True))
        pack_columns(g, l, "out", mm(low_t, att[l]))
        datt = mm(low, wout[l])
        dnum = datt * rden[l]
        dden = -dnum * att[l].astype(F32)
        for p in range(PAIRS):
            lanes = slice(128 * p, 128 * (p + 1))
            dn[p, :, 0:128] = dnum[:, lanes].astype(BF)
            dn[p, :, 128:256] = dden[:, lanes].astype(BF)
            dn_t[p] = dn[p].T
        normed_t = normed[l, 0].T
        between("pre")
        for p in range(PAIRS):
            for c in range(2):
                rows = slice(128 * c, 128 * (c + 1))
                phi_q = phi[l, 0, p, rows]
                dzq = mm(dn[p, rows], kv[l, c, p]).astype(BF) * phi_q
                store_blocks(kv.at[l, c, p], dn_t[p, :, rows], phi_q, mask)
                phi[l, 0, p, rows] = dzq
            between(f"q{p}")
        for p in range(PAIRS):
            lanes = slice(128 * p, 128 * (p + 1))
            for c in range(2):
                rows = slice(128 * c, 128 * (c + 1))
                phi_k = phi[l, 1, p, rows]
                vh = jnp.concatenate([vs[l, rows, lanes], ones_rows], axis=1)
                dzk = mm(vh, kv[l, c, p]).astype(BF) * phi_k
                dv = mm_t(phi_k, kv[l, c, p, 0:128])
                dqkv[rows, 2 * INNER + 128 * p : 2 * INNER + 128 * (p + 1)] = dv.astype(BF)
                phi[l, 1, p, rows] = dzk
            if p == PAIRS - 1:
                pack_columns(g, l, "qkv", mm(normed_t, dqkv[:, 2 * INNER :]), range(10, 15))
            between(f"k{p}")

        for side in range(2):
            b = mm_t(phi[l, side].reshape(PAIRS * 256, PAIR_W), fw[l]).reshape(PAIRS, 256, 256)
            for p in range(PAIRS):
                own = zc[l, side, p, :, 0:128].astype(F32) * TOTAL_BACK
                value = b[p, :, 0:128] * S_FEAT + b[p, :, 128:256] * own
                at = INNER * side + 128 * p
                dqkv[:, at : at + 128] = value.astype(BF)
        between("back")
        pack_columns(g, l, "qkv", mm(normed_t, dqkv[:, 0 : 2 * INNER]), range(10))
        gr2[...] = gr2[...] + norm_backward(l, 0, mm_t(dqkv[...], wqkv[l]))
        between("post")

    gr2 = x

    def turn_stream(target, s, value):
        for c in range(2):
            target[s, c] = value[SLOTS * c : SLOTS * (c + 1)].T

    for l in range(LAYERS):
        attend_forward(l)
        turn_stream(acts, 2 * l, x[...])
        mix_forward(l)
        turn_stream(acts, 2 * l + 1, x[...])
    copy_gr.wait()
    gr2[...] = jnp.concatenate([gr[0].T, gr[1].T], axis=0)
    await_greetings(10)
    act_stream.start(local_sems.at[0])
    for l in reversed(range(LAYERS)):
        mix_backward(l, lambda at: advance(DURING[l].get(at, "")))
        kept[2 * l + 1] = gr2[...]
        attend_backward(l, lambda at: advance(DURING[l].get(at, "")))
        kept[2 * l] = gr2[...]
    for n, name in enumerate(BEHIND):
        if name == "sg":
            sg_stream.forward()
        else:
            parts[name].advance()
        if n == 2:
            for turn in range(2 * LAYERS):
                turn_stream(sgrads, turn, kept[turn])
            sg_stream.start(local_sems.at[1])
            act_stream.finish()
        wire.drain(max(len(wire.sent) - 72, 0))
    sg_stream.finish()
    wire.drain(len(wire.sent))


def layers(args):
    vmem = pl.BlockSpec(memory_space=pltpu.VMEM)
    hbm = pl.BlockSpec(memory_space=pl.ANY)
    smem = pl.BlockSpec(memory_space=pltpu.SMEM)
    rows = 2 * SLOTS

    def shape(*dims):
        return jax.ShapeDtypeStruct(dims, F32)

    def share(n, *lead):
        return pltpu.VMEM(lead + (n * SHARE, 128), F32)

    scratch = [
        pltpu.VMEM((LAYERS, D, 3 * INNER), BF),
        pltpu.VMEM((LAYERS, D, INNER), BF),
        pltpu.VMEM((LAYERS, D, FF), BF),
        pltpu.VMEM((LAYERS, D, FF), BF),
        pltpu.VMEM((2, D, SLOTS), BF),
        pltpu.VMEM((rows, D), F32),
        pltpu.VMEM((2, D, SLOTS), F32),
        pltpu.VMEM((LAYERS, 2, rows, D), F32),
        pltpu.VMEM((LAYERS, 2, rows, 1), F32),
        pltpu.VMEM((LAYERS, 2, rows, D), BF),
        pltpu.VMEM((LAYERS, 256, PAIR_W), BF),
        pltpu.VMEM((LAYERS, 2, PAIRS, rows, 256), BF),
        pltpu.VMEM((LAYERS, rows, INNER), BF),
        pltpu.VMEM((INNER, rows), BF),
        pltpu.VMEM((LAYERS, 2, PAIRS, rows, PAIR_W), BF),
        pltpu.VMEM((LAYERS, 2, PAIRS, 256, PAIR_W), BF),
        pltpu.VMEM((LAYERS, rows, INNER), F32),
        pltpu.VMEM((LAYERS, rows, INNER), BF),
        pltpu.VMEM((PAIRS, rows, 256), BF),
        pltpu.VMEM((PAIRS, 256, rows), BF),
        pltpu.VMEM((rows, 3 * INNER), BF),
        pltpu.VMEM((LAYERS, rows, FF), BF),
        pltpu.VMEM((LAYERS, rows, FF), BF),
        pltpu.VMEM((2 * LAYERS, 2, D, SLOTS), F32),
        pltpu.VMEM((2 * LAYERS, 2, D, SLOTS), F32),
        pltpu.VMEM((2 * LAYERS, rows, D), F32),
        share(256),
        share(128),
        share(32),
        share(32, 3),
        share(32),
        share(8),
        share(8, 3),
        share(8, 4),
        pltpu.VMEM((2, 2, D, SLOTS), F32),
        pltpu.SemaphoreType.DMA((2 + 4 * LAYERS,)),
        pltpu.SemaphoreType.DMA((SENDS,)),
        pltpu.SemaphoreType.DMA((SENDS,)),
        pltpu.SemaphoreType.DMA((2,)),
    ]
    return pl.pallas_call(
        layers_kernel,
        out_shape=(
            pltpu.VMEM((8, D, SLOTS), F32),
            pltpu.VMEM((8, D, SLOTS), F32),
            pltpu.VMEM((256 * SHARE, 128), F32),
        ),
        in_specs=[hbm, smem, vmem, hbm, vmem, vmem, hbm, hbm, vmem, vmem, hbm, vmem, hbm, vmem],
        out_specs=(vmem, vmem, vmem),
        scratch_shapes=scratch,
        compiler_params=pltpu.CompilerParams(
            vmem_limit_bytes=53 * 1024 * 1024, collective_id=0, has_side_effects=True
        ),
        name="layers",
    )(*args)


MESH = pl.DeviceIdType.MESH

PARTS = (
    ("D0", 5, "yxz", "rqw"),
    ("D1", 3, "xyz", "rqw"),
    ("E0", 8, "xyz", "rqw"),
    ("C0", 11, "zyx", "rrw"),
    ("A0", 11, "xzy", "rqb"),
    ("F0", 8, "zyx", "rqw"),
    ("B0", 8, "yxz", "rqb"),
)
SHARE = sum(part[1] for part in PARTS)
SENDS = 21 * len(PARTS) + 12

DURING = (
    {"mix1": "A0 F0", "mix2": "C0 B0", "q0": "A0 C0 B0 F0", "k4": "E0 A0", "back": "C0 B0", "post": "E0 D0 D1 A0 F0"},
    {"mix2": "A0", "q3": "acts", "k0": "A0", "k4": "F0", "post": "B0"},
)
BEHIND = (
    "C0", "D0", "D1", "E0", "A0", "B0", "C0", "F0",
    "D0", "D1", "C0", "E0", "D0", "sg", "D1", "F0",
    "A0", "B0", "C0", "E0", "D0", "D1", "F0", "B0",
    "C0", "A0", "E0", "D0", "C0", "D1", "B0", "F0",
    "A0", "E0", "D0", "C0", "D1", "A0", "B0", "E0",
    "D0", "F0", "D1", "B0", "C0", "F0", "D0", "E0",
    "D1", "B0", "C0", "D0", "E0", "D1",
)


class Place:
    def __init__(self):
        self.dp = lax.axis_index("dp")
        self.section = lax.axis_index("section")
        self.core = lax.rem(self.dp, 2)
        self.at = {
            "x": lax.rem(self.dp // 2, 4),
            "y": self.dp // 8,
            "z": self.section,
        }

        self.ahead, self.behind = 1 + 2 * self.core, 3 - 2 * self.core
        self.steps, self.peers = {}, {}
        self.turns = {}
        for axis, at in self.at.items():
            odd = lax.rem(at, 2)
            self.turns[axis] = (1 + 2 * odd, 3 - 2 * odd)

    def step(self, axis, by):
        key = axis, by if isinstance(by, int) else id(by)
        if key not in self.steps:
            self.steps[key] = lax.rem(self.at[axis] + by, 4)
        return self.steps[key]

    def peer(self, axis, by):
        key = axis, by if isinstance(by, int) else id(by)
        if key not in self.peers:
            self.peers[key] = self.find_peer(axis, by)
        return self.peers[key]

    def find_peer(self, axis, by):
        if axis == "core":
            return {"dp": self.dp + 1 - 2 * self.core, "section": self.section}
        to = self.step(axis, by)
        if axis == "z":
            return {"dp": self.dp, "section": to}
        stride = 2 if axis == "x" else 8
        return {"dp": self.dp + stride * (to - self.at[axis]), "section": self.section}


class Wire:
    def __init__(self, send_sems, recv_sems):
        self.send_sems, self.recv_sems = send_sems, recv_sems
        self.sent = []
        self.drained = 0

    def send(self, src, dst, to):
        n = len(self.sent)
        copy = pltpu.make_async_remote_copy(
            src_ref=src,
            dst_ref=dst,
            send_sem=self.send_sems.at[n],
            recv_sem=self.recv_sems.at[n],
            device_id=to,
            device_id_type=MESH,
        )
        copy.start()
        self.sent.append(copy)
        return copy

    def drain(self, end):
        for copy in self.sent[self.drained : end]:
            copy.wait_send()
        self.drained = end


def greet(place):
    barrier = pltpu.get_barrier_semaphore()
    peers = [place.peer("core", 1)]
    peers += [place.peer(axis, by) for axis in "xyz" for by in (1, 2, 3)]
    for peer in peers:
        pl.semaphore_signal(barrier, inc=1, device_id=peer, device_id_type=MESH)


def await_greetings(count):
    pl.semaphore_wait(pltpu.get_barrier_semaphore(), count)


class Streams:
    def __init__(self, place, wire, source, target, relay):
        self.place, self.wire, self.source, self.target, self.relay = (
            place,
            wire,
            source,
            target,
            relay,
        )

    def start(self, local_sem):
        p, w = self.place, self.wire
        me, right, left, far = (p.step("z", by) for by in (0, 1, 3, 2))
        self.hops = [
            w.send(self.source.at[far, 0], self.relay.at[0], p.peer("z", 1)),
            w.send(self.source.at[far, 1], self.relay.at[1], p.peer("z", 3)),
        ]
        own = self.target.at[pl.ds(2 * me, 2)]
        self.direct = [
            w.send(self.source.at[right], own, p.peer("z", 1)),
            w.send(self.source.at[left], own, p.peer("z", 3)),
        ]
        self.local = pltpu.make_async_copy(self.source.at[me], own, local_sem)
        self.local.start()

    def forward(self):
        p, w = self.place, self.wire
        self.hops[0].wait_recv()
        self.direct.append(
            w.send(self.relay.at[0], self.target.at[2 * p.step("z", 3)], p.peer("z", 1))
        )
        self.hops[1].wait_recv()
        self.direct.append(
            w.send(self.relay.at[1], self.target.at[2 * p.step("z", 1) + 1], p.peer("z", 3))
        )

    def finish(self):
        for copy in self.direct:
            copy.wait_recv()
        self.local.wait()


class Quarters:
    def __init__(self, place, wire, axis, quarter):
        self.place, self.wire, self.axis, self.quarter = place, wire, axis, quarter

    def rows(self, by, base=0):
        start = base + self.place.step(self.axis, by) * self.quarter
        return pl.ds(pl.multiple_of(start, 8), self.quarter)

    def buffers(self, hop, near):
        self.near, self.got = near, []

    def order(self):
        return (2, 1, 3)

    def send(self, block, by):
        src, dst = block.at[self.rows(by)], self.near.at[by - 1]
        self.got.append(self.wire.send(src, dst, self.place.peer(self.axis, by)))

    def result(self, block):
        for copy in self.got:
            copy.wait_recv()
        return (block[self.rows(0), :] + self.near[0]) + (self.near[1] + self.near[2])

    def spread(self, out, base):
        view = out.at[self.rows(0, base)]
        self.back = [
            self.wire.send(view, view, self.place.peer(self.axis, by)) for by in (2, 1, 3)
        ]

    def arrivals(self):
        return zip(self.back, (2, 3, 1))

    def spread_end(self):
        for copy in self.back:
            copy.wait_recv()


class Ring:
    def __init__(self, place, wire, axis, quarter):
        self.place, self.wire, self.axis, self.quarter = place, wire, axis, quarter
        self.ahead, self.behind = place.ahead, place.behind
        self.to_ahead = place.peer(axis, self.ahead)
        self.to_behind = place.peer(axis, self.behind)

    def buffers(self, hop, near):
        self.hop, self.near = hop, near

    def order(self):
        return (2, self.behind)

    def send(self, block, by):
        src = block.at[self.rows(by)]
        if by is self.behind:
            self.got = [self.wire.send(src, self.near.at[1], self.to_behind)]
        else:
            self.far = self.wire.send(src, self.hop, self.to_ahead)

    def rows(self, by, base=0):
        start = base + self.place.step(self.axis, by) * self.quarter
        return pl.ds(pl.multiple_of(start, 8), self.quarter)

    def send_sum(self, block, more=0.0):
        self.far.wait_recv()
        self.hop[...] = (self.hop[...] + block[self.rows(self.ahead), :]) + more
        self.got.append(self.wire.send(self.hop, self.near.at[0], self.to_ahead))

    def result(self, block):
        for copy in self.got:
            copy.wait_recv()
        return block[self.rows(0), :] + self.near[0] + self.near[1]

    def spread(self, out, base):
        w = self.wire
        view = out.at[self.rows(0, base)]
        self.first = w.send(view, view, self.to_ahead)
        self.others = [w.send(view, view, self.to_behind)]

    def spread_on(self, out, base):
        self.first.wait_recv()
        view = out.at[self.rows(self.behind, base)]
        self.others.append(self.wire.send(view, view, self.to_ahead))

    def arrivals(self):
        return zip(self.others, (self.ahead, 2))

    def spread_end(self):
        for copy in self.others:
            copy.wait_recv()


class Part:
    def __init__(self, place, wire, tiles, axes, kind, before, g, out, bufs):
        self.place, self.wire, self.axes, self.g, self.out = place, wire, axes, g, out
        t, b = tiles, before
        self.t, self.b = t, b
        base, core = 256 * b, place.core
        self.mine = pl.multiple_of(base + core * (128 * t), 8)
        self.other = pl.multiple_of(base + (1 - core) * (128 * t), 8)
        self.at1 = self.mine + place.at[axes[0]] * (32 * t)
        self.at2 = self.at1 + place.at[axes[1]] * (8 * t)
        own, hop1, near1, t1, hop2, near2, last = bufs
        self.own_all = own
        self.own = own.at[self.spot(128)]
        self.t1 = t1.at[self.spot(32)]
        self.last = last.at[:, self.spot(8)]
        self.phase1 = (Ring if kind[0] == "r" else Quarters)(place, wire, axes[0], 32 * t)
        self.phase1.buffers(hop1.at[self.spot(32)], near1.at[:, self.spot(32)])
        self.phase2 = (Ring if kind[1] == "r" else Quarters)(place, wire, axes[1], 8 * t)
        self.phase2.buffers(hop2.at[self.spot(8)], near2.at[:, self.spot(8)])
        self.whole = kind[2] == "w"
        self.at = 0
        self.steps = [self.swap, self.join]
        if kind[0] == "r":
            self.steps.append(self.sums)
        self.steps.append(self.second)
        if kind[1] == "r":
            self.steps.append(self.second_sums)
        self.steps.append(self.third)
        if not self.whole:
            self.steps.append(self.third_again)
        self.steps.append(self.total)
        if kind[1] == "r":
            self.steps.append(self.back2_on)
        self.steps.append(self.back1)
        if kind[0] == "r":
            self.steps.append(self.back1_on)
        self.steps += [self.give_rest, self.taken]

    def advance(self):
        self.steps[self.at]()
        self.at += 1

    def spot(self, rows):
        return pl.ds(rows * self.b, rows * self.t)

    def swap(self):
        src = self.g.at[pl.ds(self.other, 128 * self.t)]
        self.swapped = self.wire.send(src, self.own, self.place.peer("core", 1))

    def add_quarter(self, by):
        rows = 32 * self.t
        start = self.place.step(self.axes[0], by) * rows
        to = pl.ds(pl.multiple_of(128 * self.b + start, 8), rows)
        mine = pl.ds(pl.multiple_of(self.mine + start, 8), rows)
        self.own_all[to, :] = self.own_all[to, :] + self.g[mine, :]

    def join(self):
        self.swapped.wait_recv()
        for by in self.phase1.order():
            self.add_quarter(by)
            self.phase1.send(self.own, by)

    def rest(self, by):
        start = self.place.step(self.axes[0], by) * (32 * self.t)
        return self.g[pl.ds(pl.multiple_of(self.mine + start, 8), 32 * self.t), :]

    def sums(self):
        self.phase1.send_sum(self.own, self.rest(self.place.ahead))

    def second(self):
        self.t1[...] = self.phase1.result(self.own) + self.rest(0)
        for by in self.phase2.order():
            self.phase2.send(self.t1, by)

    def second_sums(self):
        self.phase2.send_sum(self.t1)

    def third(self):
        axis = self.axes[2]
        value = self.phase2.result(self.t1)
        if self.whole:
            here = self.place.at[axis]
            self.last[here] = value
            view = self.last.at[here]
            self.thirds = [
                self.wire.send(view, view, self.place.peer(axis, by)) for by in (2, 1, 3)
            ]
        else:
            self.last[0] = value
            to = self.place.peer(axis, self.place.turns[axis][0])
            self.thirds = [self.wire.send(self.last.at[0], self.last.at[1], to)]

    def third_again(self):
        self.thirds[0].wait_recv()
        self.last[2] = self.last[0] + self.last[1]
        to = self.place.peer(self.axes[2], self.place.turns[self.axes[2]][1])
        self.thirds = [self.wire.send(self.last.at[2], self.last.at[3], to)]

    def total(self):
        for copy in self.thirds:
            copy.wait_recv()
        z = self.last
        rows = pl.ds(pl.multiple_of(self.at2, 8), 8 * self.t)
        if self.whole:
            self.out[rows, :] = (z[0] + z[1]) + (z[2] + z[3])
        else:
            self.out[rows, :] = z[2] + z[3]
        self.phase2.spread(self.out, self.at1)

    def back2_on(self):
        self.phase2.spread_on(self.out, self.at1)

    def back1(self):
        self.phase2.spread_end()
        self.phase1.spread(self.out, self.mine)
        self.given = []
        self.give(0)

    def back1_on(self):
        self.phase1.spread_on(self.out, self.mine)
        self.give(self.place.behind)

    def give(self, by):
        view = self.out.at[self.phase1.rows(by, self.mine)]
        self.given.append(self.wire.send(view, view, self.place.peer("core", 1)))

    def give_rest(self):
        for copy, by in self.phase1.arrivals():
            copy.wait_recv()
            self.give(by)

    def taken(self):
        for copy in self.given:
            copy.wait_recv()


def finish_kernel(
    acts,
    sgrads,
    out,
    acts_out,
    sg_out,
    gains,
    shifts,
    qkv_out,
    out_out,
    bout,
    up_out,
    bup,
    down_out,
    bdown,
    qkv,
    out_w,
    up,
    down,
    sems,
):
    copies = []

    def start(src, dst):
        copies.append(pltpu.make_async_copy(src, dst, sems.at[len(copies)]))
        copies[-1].start()

    start(acts, acts_out)
    start(sgrads, sg_out)
    for l in range(LAYERS):
        for kind, target, result, width in (
            ("qkv", qkv, qkv_out, 3 * INNER),
            ("out", out_w, out_out, INNER),
            ("up", up, up_out, FF),
            ("down", down, down_out, FF),
        ):
            for j in range(pl.cdiv(width, 128)):
                take = min(128, width - 128 * j)
                at = ROWS[l, kind, j]
                target[l, :, 128 * j : 128 * j + take] = out[at : at + COL, 0:take]
            start(target.at[l], result.at[l])
    write_small(out, gains, shifts, bout, bup, bdown)
    for copy in copies:
        copy.wait()


def finish(acts, sgrads, out):
    vmem = pl.BlockSpec(memory_space=pltpu.VMEM)
    hbm = pl.BlockSpec(memory_space=pl.ANY)

    def shape(*dims):
        return jax.ShapeDtypeStruct(dims, F32)

    return pl.pallas_call(
        finish_kernel,
        out_shape=(
            shape(8, D, SLOTS),
            shape(8, D, SLOTS),
            shape(LAYERS, 2, D),
            shape(LAYERS, 2, D),
            shape(LAYERS, D, 3 * INNER),
            shape(LAYERS, D, INNER),
            shape(LAYERS, D),
            shape(LAYERS, D, FF),
            shape(LAYERS, FF),
            shape(LAYERS, D, FF),
            shape(LAYERS, D),
        ),
        in_specs=[vmem, vmem, vmem],
        out_specs=(hbm, hbm, vmem, vmem, hbm, hbm, vmem, hbm, vmem, hbm, vmem),
        scratch_shapes=[
            pltpu.VMEM((LAYERS, D, 3 * INNER), F32),
            pltpu.VMEM((LAYERS, D, INNER), F32),
            pltpu.VMEM((LAYERS, D, FF), F32),
            pltpu.VMEM((LAYERS, D, FF), F32),
            pltpu.SemaphoreType.DMA((2 + 4 * LAYERS,)),
        ],
        compiler_params=pltpu.CompilerParams(vmem_limit_bytes=24 * 1024 * 1024),
        name="finish",
    )(acts, sgrads, out)


def write_small(out, gains, shifts, bout, bup, bdown):
    for l in range(LAYERS):

        def row(at, width):
            start = SMALL_ROW[l] + at
            rows = [out[start + j : start + j + 1, :] for j in range(pl.cdiv(width, 128))]
            return jnp.concatenate(rows, axis=1)[:, 0:width]

        for j in range(2):
            gains[l, j : j + 1, :] = row(7 + 2 * j, D)
            shifts[l, j : j + 1, :] = row(11 + 2 * j, D)
        bout[l : l + 1, :] = row(15, D)
        bup[l : l + 1, :] = row(0, FF)
        bdown[l : l + 1, :] = row(17, D)


def body(
    inputs,
    lengths,
    gene_mask,
    out_grad,
    gain,
    bias,
    wqkv,
    wout,
    bout,
    feats,
    wup,
    bup,
    wdown,
    bdown,
):
    def flip(value):
        return jnp.swapaxes(value, -1, -2)

    streams_and_sums = layers(
        (
            flip(inputs),
            lengths,
            gene_mask,
            flip(out_grad),
            gain,
            bias,
            wqkv,
            flip(wout),
            bout,
            feats,
            wup,
            bup,
            flip(wdown),
            bdown,
        )
    )
    acts, sgrads, gains, shifts, qkv, out, dbout, up, dbup, down, dbdown = finish(*streams_and_sums)
    return (
        flip(acts)[None],
        flip(sgrads)[None],
        gains,
        shifts,
        qkv,
        flip(out),
        dbout,
        up,
        dbup,
        flip(down),
        dbdown,
    )


def solution(mesh):
    placed = (
        P("dp", None, None),
        P("dp"),
        P("dp", None),
        P("dp", None, None),
    ) + (P(),) * 10
    return jax.shard_map(
        body,
        mesh=mesh,
        in_specs=placed,
        out_specs=(P("section", "dp", None, None),) * 2 + (P(),) * 9,
        check_vma=False,
    )
```

```python
import math

import jax
import jax.numpy as jnp
from jax import lax
from jax.experimental import pallas as pl
from jax.experimental.pallas import tpu as pltpu
from jax.sharding import PartitionSpec as P

D = 200
HEADS = 10
HEAD_DIM = 64
FEATS = 266
FF = 800
INNER = HEADS * HEAD_DIM
LAYERS = 2
SLOTS = 128
EPSILON = 1e-05

PAIRS = HEADS // 2
MAIN = 256
TAIL = FEATS - MAIN
PAIR_W = 2 * MAIN + 128

LOG2E = math.log2(math.e)
S_FEAT = HEAD_DIM ** (-0.25)
S_NORM = HEAD_DIM ** (-0.5)
Q_SCALE = S_FEAT * LOG2E
SQ_SCALE = 0.5 * S_NORM * LOG2E
SQ_SHIFT = 0.5 * math.log2(FEATS) / HEAD_DIM
MASK_SHIFT = 1000.0
TOTAL_BACK = S_NORM / Q_SCALE

COL = 200
QK = [("qkv", j) for j in range(10)]
OUT_V = [("out", j) for j in range(5)] + [("qkv", j) for j in range(10, 15)]
UP_DOWN = [("up", j) for j in range(7)] + [("down", j) for j in range(7)]
D_ROW, E_ROW, C_ROW, A_ROW, F_ROW, B_ROW, G_ROWS = 0, 2048, 4096, 6912, 9728, 11776, 13824


def place_columns():
    rows = {}

    def put(l, columns, at):
        for column in columns:
            rows[(l,) + column] = at
            at += COL
        return at

    ends = [
        put(0, QK, D_ROW) + 24,
        put(0, OUT_V, E_ROW),
        put(0, UP_DOWN, C_ROW),
        put(1, UP_DOWN, A_ROW),
        put(1, OUT_V, F_ROW),
        put(1, QK, B_ROW) + 24,
    ]
    return rows, ends


ROWS, ENDS = place_columns()
SMALL_ROW = (ENDS[0] - 24, ENDS[5] - 24)

BF = jnp.bfloat16
F32 = jnp.float32


def mm(a, b):
    return jnp.dot(a, b, preferred_element_type=F32)


def mm_t(a, b):
    return lax.dot_general(a, b, (((1,), (1,)), ((), ())), preferred_element_type=F32)


def norm_forward(rows):
    centered = rows - jnp.mean(rows, axis=-1, keepdims=True)
    inverse = lax.rsqrt(jnp.mean(centered * centered, axis=-1, keepdims=True) + EPSILON)
    return centered * inverse, inverse


def normal_cdf(value, bell):
    base = 1.0 + 0.3275911 * math.sqrt(0.5) * jnp.abs(value)
    guess = pl.reciprocal(base, approx=True)
    t = guess * (2.0 - base * guess)
    poly = 1.061405429
    for factor in (-1.453152027, 1.421413741, -0.284496736, 0.254829592):
        poly = poly * t + factor
    tail = 0.5 * poly * t * bell
    return jnp.where(value < 0.0, tail, 1.0 - tail)


def build_maps(feats_ref, fw):
    ones = jnp.full((HEAD_DIM, MAIN), -1.0, BF)
    row = lax.broadcasted_iota(jnp.int32, (FEATS, 128), 0)
    lane = lax.broadcasted_iota(jnp.int32, (FEATS, 128), 1)
    tail_lane = lax.broadcasted_iota(jnp.int32, (HEAD_DIM, 128), 1)
    for l in range(LAYERS):
        f = feats_ref[l]
        fw[l, :, 0 : 2 * MAIN] = jnp.zeros((256, 2 * MAIN), BF)
        for hh in range(2):
            pick = jnp.where(row - MAIN == lane - TAIL * hh, 1.0, 0.0)
            pick = jnp.where(row >= MAIN, pick, 0.0).astype(BF)
            tail = mm(f, pick).astype(BF)
            minus = jnp.where(
                (tail_lane >= TAIL * hh) & (tail_lane < TAIL * (hh + 1)), -1.0, 0.0
            ).astype(BF)
            r = HEAD_DIM * hh
            fw[l, r : r + HEAD_DIM, MAIN * hh : MAIN * (hh + 1)] = f[:, 0:MAIN]
            fw[l, 128 + r : 128 + r + HEAD_DIM, MAIN * hh : MAIN * (hh + 1)] = ones
            fw[l, r : r + HEAD_DIM, 2 * MAIN : PAIR_W] = tail
            fw[l, 128 + r : 128 + r + HEAD_DIM, 2 * MAIN : PAIR_W] = minus


def tail_mask():
    row = lax.broadcasted_iota(jnp.int32, (256, 128), 0)
    lane = lax.broadcasted_iota(jnp.int32, (256, 128), 1)
    odd = (row % 128) >= HEAD_DIM
    low = jnp.where(odd, TAIL, 0)
    return jnp.where((lane >= low) & (lane < low + TAIL), 1.0, 0.0)


def store_blocks(target, left, right, mask):
    for hh in range(2):
        r = HEAD_DIM * hh
        lhs = jnp.concatenate(
            [left[r : r + HEAD_DIM], left[128 + r : 128 + r + HEAD_DIM]], axis=0
        )
        block = mm(lhs, right[:, MAIN * hh : MAIN * (hh + 1)]).astype(BF)
        target[r : r + HEAD_DIM, MAIN * hh : MAIN * (hh + 1)] = block[0:HEAD_DIM]
        target[128 + r : 128 + r + HEAD_DIM, MAIN * hh : MAIN * (hh + 1)] = block[HEAD_DIM:]
    target[:, 2 * MAIN : PAIR_W] = (mm(left, right[:, 2 * MAIN : PAIR_W]) * mask).astype(BF)


def pack_columns(g, l, kind, value, columns=None):
    width = value.shape[1]
    columns = range(pl.cdiv(width, 128)) if columns is None else columns
    for n, j in enumerate(columns):
        take = min(128, width - 128 * n)
        at = ROWS[l, kind, j]
        g[at : at + COL, 0:take] = value[:, 128 * n : 128 * n + take]


def pack_row(g, l, row, value):
    width = value.shape[1]
    for j in range(pl.cdiv(width, 128)):
        take = min(128, width - 128 * j)
        at = SMALL_ROW[l] + row + j
        g[at : at + 1, 0:take] = value[:, 128 * j : 128 * j + take]


def clear_gaps(g):
    def clear(start, end):
        if end > start:
            g[start:end, :] = jnp.zeros((end - start, 128), F32)

    for end, limit in zip(ENDS, (E_ROW, C_ROW, A_ROW, F_ROW, B_ROW, G_ROWS)):
        clear(end, limit)
    for l in range(LAYERS):
        clear(SMALL_ROW[l], SMALL_ROW[l] + 24)
        for kind in ("up", "down"):
            clear(ROWS[l, kind, 6], ROWS[l, kind, 6] + COL)


def layers_kernel(
    inputs_hbm,
    lengths,
    gene_mask,
    out_grad_hbm,
    gain,
    bias,
    wqkv_hbm,
    wout_hbm,
    bout,
    feats,
    wup_hbm,
    bup,
    wdown_hbm,
    bdown,
    acts_out,
    sg_out,
    out,
    wqkv,
    wout,
    wup,
    wdown,
    x_in,
    x,
    gr,
    xhat,
    inv,
    normed,
    fw,
    zc,
    vs,
    vt,
    phi,
    kv,
    rden,
    att,
    dn,
    dn_t,
    dqkv,
    hid,
    gp,
    acts,
    sgrads,
    kept,
    g,
    own,
    hop1,
    near1,
    t1,
    hop2,
    near2,
    last,
    relay,
    sems,
    send_sems,
    recv_sems,
    local_sems,
):
    place = Place()
    wire = Wire(send_sems, recv_sems)
    greet(place)
    parts, before = {}, 0
    for name, t, axes, kind in PARTS:
        bufs = (own, hop1, near1, t1, hop2, near2, last)
        parts[name] = Part(place, wire, t, axes, kind, before, g, out, bufs)
        before += t
    act_stream = Streams(place, wire, acts, acts_out, relay.at[0])
    sg_stream = Streams(place, wire, sgrads, sg_out, relay.at[1])

    def advance(names):
        for name in names.split():
            if name == "acts":
                act_stream.forward()
            else:
                parts[name].advance()

    section = lax.axis_index("section")
    first = section * 2
    copy_in = pltpu.make_async_copy(inputs_hbm.at[pl.ds(first, 2)], x_in, sems.at[0])
    copy_gr = pltpu.make_async_copy(out_grad_hbm.at[pl.ds(first, 2)], gr, sems.at[1])
    copy_in.start()
    loads = {}
    for l in range(LAYERS):
        for n, (name, src, dst) in enumerate(
            (
                ("qkv", wqkv_hbm, wqkv),
                ("out", wout_hbm, wout),
                ("up", wup_hbm, wup),
                ("down", wdown_hbm, wdown),
            )
        ):
            loads[name, l] = pltpu.make_async_copy(src.at[l], dst.at[l], sems.at[2 + 4 * l + n])
            loads[name, l].start()
    copy_gr.start()
    build_maps(feats, fw)
    mask = tail_mask()
    ones_rows = jnp.ones((128, 128), BF)

    blank = jnp.zeros((LAYERS, 2, PAIRS, HEAD_DIM, MAIN), BF)
    for r in range(4):
        side = MAIN * (1 - r % 2)
        kv[:, :, :, HEAD_DIM * r : HEAD_DIM * (r + 1), side : side + MAIN] = blank
    clear_gaps(g)

    slot = lax.broadcasted_iota(jnp.int32, (128, 128), 1)
    shift = []
    for c in range(2):
        marks = jnp.broadcast_to(gene_mask[pl.ds(first + c, 1), :], (128, 128))
        live = (slot < lengths[first + c]) & (marks > 0)
        shift.append(jnp.where(live, SQ_SHIFT, MASK_SHIFT).T)
    key_shift = jnp.concatenate(shift, axis=0)

    copy_in.wait()
    x[...] = jnp.concatenate([x_in[0].T, x_in[1].T], axis=0).astype(F32)

    def attend_forward(l):
        nx, iv = norm_forward(x[...])
        xhat[l, 0] = nx
        inv[l, 0] = iv
        nb = (nx * gain[l, 0:1] + bias[l, 0:1]).astype(BF)
        normed[l, 0] = nb
        loads["qkv", l].wait()
        for side, shift in ((0, SQ_SHIFT), (1, key_shift)):
            value = mm(nb, wqkv[l, :, INNER * side : INNER * (side + 1)])
            for p in range(PAIRS):
                part = value[:, 128 * p : 128 * (p + 1)]
                zc[l, side, p, :, 0:128] = (part * Q_SCALE).astype(BF)
                zc[l, side, p, :, 128:256] = (part * part * SQ_SCALE + shift).astype(BF)
        v = mm(nb, wqkv[l, :, 2 * INNER : 3 * INNER]).astype(BF)
        vs[l] = v
        vt[...] = v.T

        for side in range(2):
            z = mm(zc[l, side].reshape(PAIRS * 256, 256), fw[l])
            phi[l, side] = jnp.exp2(z).astype(BF).reshape(PAIRS, 256, PAIR_W)
        for p in range(PAIRS):
            for c in range(2):
                rows = slice(128 * c, 128 * (c + 1))
                left = jnp.concatenate([vt[128 * p : 128 * (p + 1), rows], ones_rows], axis=0)
                store_blocks(kv.at[l, c, p], left, phi[l, 1, p, rows], mask)
        for p in range(PAIRS):
            lanes = slice(128 * p, 128 * (p + 1))
            for c in range(2):
                rows = slice(128 * c, 128 * (c + 1))
                nd = mm_t(phi[l, 0, p, rows], kv[l, c, p])
                rd = 1.0 / nd[:, 128:]
                rden[l, rows, lanes] = rd
                att[l, rows, lanes] = (nd[:, 0:128] * rd).astype(BF)
        loads["out", l].wait()
        x[...] = x[...] + mm_t(att[l], wout[l]) + bout[l : l + 1]

    def mix_forward(l):
        nx, iv = norm_forward(x[...])
        xhat[l, 1] = nx
        inv[l, 1] = iv
        nb = (nx * gain[l, 1:2] + bias[l, 1:2]).astype(BF)
        normed[l, 1] = nb
        loads["up", l].wait()
        loads["down", l].wait()
        pre = mm(nb, wup[l]) + bup[l : l + 1]
        bell = jnp.exp2(pre * pre * (-0.5 * LOG2E))
        cdf = normal_cdf(pre, bell)
        hid[l] = (pre * cdf).astype(BF)
        gp[l] = (cdf + pre * bell * (1.0 / math.sqrt(2.0 * math.pi))).astype(BF)
        x[...] = x[...] + mm_t(hid[l], wdown[l]) + bdown[l : l + 1]

    def norm_backward(l, j, grad_normed):
        nx = xhat[l, j]
        pack_row(g, l, 7 + 2 * j, jnp.sum(grad_normed * nx, axis=0, keepdims=True))
        pack_row(g, l, 11 + 2 * j, jnp.sum(grad_normed, axis=0, keepdims=True))
        scaled = grad_normed * gain[l, j : j + 1]
        return inv[l, j] * (
            scaled
            - jnp.mean(scaled, axis=-1, keepdims=True)
            - nx * jnp.mean(scaled * nx, axis=-1, keepdims=True)
        )

    def mix_backward(l, between):
        low = gr2[...].astype(BF)
        low_t = low.T
        pack_row(g, l, 17, jnp.sum(low.astype(F32), axis=0, keepdims=True))
        pack_columns(g, l, "down", mm(low_t, hid[l]))
        between("mix0")
        dpre = (mm(low, wdown[l]) * gp[l].astype(F32)).astype(BF)
        pack_row(g, l, 0, jnp.sum(dpre.astype(F32), axis=0, keepdims=True))
        between("mix1")
        pack_columns(g, l, "up", mm(normed[l, 1].T, dpre))
        between("mix2")
        gr2[...] = gr2[...] + norm_backward(l, 1, mm_t(dpre, wup[l]))
        between("mix3")

    def attend_backward(l, between):
        low = gr2[...].astype(BF)
        low_t = low.T
        pack_row(g, l, 15, jnp.sum(low.astype(F32), axis=0, keepdims=True))
        pack_columns(g, l, "out", mm(low_t, att[l]))
        datt = mm(low, wout[l])
        dnum = datt * rden[l]
        dden = -dnum * att[l].astype(F32)
        for p in range(PAIRS):
            lanes = slice(128 * p, 128 * (p + 1))
            dn[p, :, 0:128] = dnum[:, lanes].astype(BF)
            dn[p, :, 128:256] = dden[:, lanes].astype(BF)
            dn_t[p] = dn[p].T
        normed_t = normed[l, 0].T
        between("pre")
        for p in range(PAIRS):
            for c in range(2):
                rows = slice(128 * c, 128 * (c + 1))
                phi_q = phi[l, 0, p, rows]
                dzq = mm(dn[p, rows], kv[l, c, p]).astype(BF) * phi_q
                store_blocks(kv.at[l, c, p], dn_t[p, :, rows], phi_q, mask)
                phi[l, 0, p, rows] = dzq
            between(f"q{p}")
        for p in range(PAIRS):
            lanes = slice(128 * p, 128 * (p + 1))
            for c in range(2):
                rows = slice(128 * c, 128 * (c + 1))
                phi_k = phi[l, 1, p, rows]
                vh = jnp.concatenate([vs[l, rows, lanes], ones_rows], axis=1)
                dzk = mm(vh, kv[l, c, p]).astype(BF) * phi_k
                dv = mm_t(phi_k, kv[l, c, p, 0:128])
                dqkv[rows, 2 * INNER + 128 * p : 2 * INNER + 128 * (p + 1)] = dv.astype(BF)
                phi[l, 1, p, rows] = dzk
            if p == PAIRS - 1:
                pack_columns(g, l, "qkv", mm(normed_t, dqkv[:, 2 * INNER :]), range(10, 15))
            between(f"k{p}")

        for side in range(2):
            b = mm_t(phi[l, side].reshape(PAIRS * 256, PAIR_W), fw[l]).reshape(PAIRS, 256, 256)
            for p in range(PAIRS):
                own = zc[l, side, p, :, 0:128].astype(F32) * TOTAL_BACK
                value = b[p, :, 0:128] * S_FEAT + b[p, :, 128:256] * own
                at = INNER * side + 128 * p
                dqkv[:, at : at + 128] = value.astype(BF)
        between("back")
        pack_columns(g, l, "qkv", mm(normed_t, dqkv[:, 0 : 2 * INNER]), range(10))
        gr2[...] = gr2[...] + norm_backward(l, 0, mm_t(dqkv[...], wqkv[l]))
        between("post")

    gr2 = x

    def turn_stream(target, s, value):
        for c in range(2):
            target[s, c] = value[SLOTS * c : SLOTS * (c + 1)].T

    for l in range(LAYERS):
        attend_forward(l)
        turn_stream(acts, 2 * l, x[...])
        mix_forward(l)
        turn_stream(acts, 2 * l + 1, x[...])
    copy_gr.wait()
    gr2[...] = jnp.concatenate([gr[0].T, gr[1].T], axis=0)
    await_greetings(10)
    act_stream.start(local_sems.at[0])
    for l in reversed(range(LAYERS)):
        mix_backward(l, lambda at: advance(DURING[l].get(at, "")))
        kept[2 * l + 1] = gr2[...]
        attend_backward(l, lambda at: advance(DURING[l].get(at, "")))
        kept[2 * l] = gr2[...]
    for n, name in enumerate(BEHIND):
        if name == "sg":
            sg_stream.forward()
        else:
            parts[name].advance()
        if n == 2:
            for turn in range(2 * LAYERS):
                turn_stream(sgrads, turn, kept[turn])
            sg_stream.start(local_sems.at[1])
            act_stream.finish()
        wire.drain(max(len(wire.sent) - 72, 0))
    sg_stream.finish()
    wire.drain(len(wire.sent))


def layers(args):
    vmem = pl.BlockSpec(memory_space=pltpu.VMEM)
    hbm = pl.BlockSpec(memory_space=pl.ANY)
    smem = pl.BlockSpec(memory_space=pltpu.SMEM)
    rows = 2 * SLOTS

    def shape(*dims):
        return jax.ShapeDtypeStruct(dims, F32)

    def share(n, *lead):
        return pltpu.VMEM(lead + (n * SHARE, 128), F32)

    scratch = [
        pltpu.VMEM((LAYERS, D, 3 * INNER), BF),
        pltpu.VMEM((LAYERS, D, INNER), BF),
        pltpu.VMEM((LAYERS, D, FF), BF),
        pltpu.VMEM((LAYERS, D, FF), BF),
        pltpu.VMEM((2, D, SLOTS), BF),
        pltpu.VMEM((rows, D), F32),
        pltpu.VMEM((2, D, SLOTS), F32),
        pltpu.VMEM((LAYERS, 2, rows, D), F32),
        pltpu.VMEM((LAYERS, 2, rows, 1), F32),
        pltpu.VMEM((LAYERS, 2, rows, D), BF),
        pltpu.VMEM((LAYERS, 256, PAIR_W), BF),
        pltpu.VMEM((LAYERS, 2, PAIRS, rows, 256), BF),
        pltpu.VMEM((LAYERS, rows, INNER), BF),
        pltpu.VMEM((INNER, rows), BF),
        pltpu.VMEM((LAYERS, 2, PAIRS, rows, PAIR_W), BF),
        pltpu.VMEM((LAYERS, 2, PAIRS, 256, PAIR_W), BF),
        pltpu.VMEM((LAYERS, rows, INNER), F32),
        pltpu.VMEM((LAYERS, rows, INNER), BF),
        pltpu.VMEM((PAIRS, rows, 256), BF),
        pltpu.VMEM((PAIRS, 256, rows), BF),
        pltpu.VMEM((rows, 3 * INNER), BF),
        pltpu.VMEM((LAYERS, rows, FF), BF),
        pltpu.VMEM((LAYERS, rows, FF), BF),
        pltpu.VMEM((2 * LAYERS, 2, D, SLOTS), F32),
        pltpu.VMEM((2 * LAYERS, 2, D, SLOTS), F32),
        pltpu.VMEM((2 * LAYERS, rows, D), F32),
        share(256),
        share(128),
        share(32),
        share(32, 3),
        share(32),
        share(8),
        share(8, 3),
        share(8, 4),
        pltpu.VMEM((2, 2, D, SLOTS), F32),
        pltpu.SemaphoreType.DMA((2 + 4 * LAYERS,)),
        pltpu.SemaphoreType.DMA((SENDS,)),
        pltpu.SemaphoreType.DMA((SENDS,)),
        pltpu.SemaphoreType.DMA((2,)),
    ]
    return pl.pallas_call(
        layers_kernel,
        out_shape=(
            pltpu.VMEM((8, D, SLOTS), F32),
            pltpu.VMEM((8, D, SLOTS), F32),
            pltpu.VMEM((256 * SHARE, 128), F32),
        ),
        in_specs=[hbm, smem, vmem, hbm, vmem, vmem, hbm, hbm, vmem, vmem, hbm, vmem, hbm, vmem],
        out_specs=(vmem, vmem, vmem),
        scratch_shapes=scratch,
        compiler_params=pltpu.CompilerParams(
            vmem_limit_bytes=53 * 1024 * 1024, collective_id=0, has_side_effects=True
        ),
        name="layers",
    )(*args)


MESH = pl.DeviceIdType.MESH

PARTS = (
    ("D0", 5, "yxz", "rqw"),
    ("D1", 3, "xyz", "rqw"),
    ("E0", 8, "xyz", "rqw"),
    ("C0", 11, "zyx", "rrw"),
    ("A0", 11, "xzy", "rqb"),
    ("F0", 8, "zyx", "rqw"),
    ("B0", 8, "yxz", "rqb"),
)
SHARE = sum(part[1] for part in PARTS)
SENDS = 21 * len(PARTS) + 12

DURING = (
    {"mix1": "A0 F0", "mix2": "C0 B0", "q0": "A0 C0 B0 F0", "k4": "E0 A0", "back": "C0 B0", "post": "E0 D0 D1 A0 F0"},
    {"mix2": "A0", "q3": "acts", "k0": "A0", "k4": "F0", "post": "B0"},
)
BEHIND = (
    "C0", "D0", "D1", "E0", "A0", "B0", "C0", "F0",
    "D0", "D1", "C0", "E0", "D0", "sg", "D1", "F0",
    "A0", "B0", "C0", "E0", "D0", "D1", "F0", "B0",
    "C0", "A0", "E0", "D0", "C0", "D1", "B0", "F0",
    "A0", "E0", "D0", "C0", "D1", "A0", "B0", "E0",
    "D0", "F0", "D1", "B0", "C0", "F0", "D0", "E0",
    "D1", "B0", "C0", "D0", "E0", "D1",
)


class Place:
    def __init__(self):
        self.dp = lax.axis_index("dp")
        self.section = lax.axis_index("section")
        self.core = lax.rem(self.dp, 2)
        self.at = {
            "x": lax.rem(self.dp // 2, 4),
            "y": self.dp // 8,
            "z": self.section,
        }

        self.ahead, self.behind = 1 + 2 * self.core, 3 - 2 * self.core
        self.steps, self.peers = {}, {}
        self.turns = {}
        for axis, at in self.at.items():
            odd = lax.rem(at, 2)
            self.turns[axis] = (1 + 2 * odd, 3 - 2 * odd)

    def step(self, axis, by):
        key = axis, by if isinstance(by, int) else id(by)
        if key not in self.steps:
            self.steps[key] = lax.rem(self.at[axis] + by, 4)
        return self.steps[key]

    def peer(self, axis, by):
        key = axis, by if isinstance(by, int) else id(by)
        if key not in self.peers:
            self.peers[key] = self.find_peer(axis, by)
        return self.peers[key]

    def find_peer(self, axis, by):
        if axis == "core":
            return {"dp": self.dp + 1 - 2 * self.core, "section": self.section}
        to = self.step(axis, by)
        if axis == "z":
            return {"dp": self.dp, "section": to}
        stride = 2 if axis == "x" else 8
        return {"dp": self.dp + stride * (to - self.at[axis]), "section": self.section}


class Wire:
    def __init__(self, send_sems, recv_sems):
        self.send_sems, self.recv_sems = send_sems, recv_sems
        self.sent = []
        self.drained = 0

    def send(self, src, dst, to):
        n = len(self.sent)
        copy = pltpu.make_async_remote_copy(
            src_ref=src,
            dst_ref=dst,
            send_sem=self.send_sems.at[n],
            recv_sem=self.recv_sems.at[n],
            device_id=to,
            device_id_type=MESH,
        )
        copy.start()
        self.sent.append(copy)
        return copy

    def drain(self, end):
        for copy in self.sent[self.drained : end]:
            copy.wait_send()
        self.drained = end


def greet(place):
    barrier = pltpu.get_barrier_semaphore()
    peers = [place.peer("core", 1)]
    peers += [place.peer(axis, by) for axis in "xyz" for by in (1, 2, 3)]
    for peer in peers:
        pl.semaphore_signal(barrier, inc=1, device_id=peer, device_id_type=MESH)


def await_greetings(count):
    pl.semaphore_wait(pltpu.get_barrier_semaphore(), count)


class Streams:
    def __init__(self, place, wire, source, target, relay):
        self.place, self.wire, self.source, self.target, self.relay = (
            place,
            wire,
            source,
            target,
            relay,
        )

    def start(self, local_sem):
        p, w = self.place, self.wire
        me, right, left, far = (p.step("z", by) for by in (0, 1, 3, 2))
        self.hops = [
            w.send(self.source.at[far, 0], self.relay.at[0], p.peer("z", 1)),
            w.send(self.source.at[far, 1], self.relay.at[1], p.peer("z", 3)),
        ]
        own = self.target.at[pl.ds(2 * me, 2)]
        self.direct = [
            w.send(self.source.at[right], own, p.peer("z", 1)),
            w.send(self.source.at[left], own, p.peer("z", 3)),
        ]
        self.local = pltpu.make_async_copy(self.source.at[me], own, local_sem)
        self.local.start()

    def forward(self):
        p, w = self.place, self.wire
        self.hops[0].wait_recv()
        self.direct.append(
            w.send(self.relay.at[0], self.target.at[2 * p.step("z", 3)], p.peer("z", 1))
        )
        self.hops[1].wait_recv()
        self.direct.append(
            w.send(self.relay.at[1], self.target.at[2 * p.step("z", 1) + 1], p.peer("z", 3))
        )

    def finish(self):
        for copy in self.direct:
            copy.wait_recv()
        self.local.wait()


class Quarters:
    def __init__(self, place, wire, axis, quarter):
        self.place, self.wire, self.axis, self.quarter = place, wire, axis, quarter

    def rows(self, by, base=0):
        start = base + self.place.step(self.axis, by) * self.quarter
        return pl.ds(pl.multiple_of(start, 8), self.quarter)

    def buffers(self, hop, near):
        self.near, self.got = near, []

    def order(self):
        return (2, 1, 3)

    def send(self, block, by):
        src, dst = block.at[self.rows(by)], self.near.at[by - 1]
        self.got.append(self.wire.send(src, dst, self.place.peer(self.axis, by)))

    def result(self, block):
        for copy in self.got:
            copy.wait_recv()
        return (block[self.rows(0), :] + self.near[0]) + (self.near[1] + self.near[2])

    def spread(self, out, base):
        view = out.at[self.rows(0, base)]
        self.back = [
            self.wire.send(view, view, self.place.peer(self.axis, by)) for by in (2, 1, 3)
        ]

    def arrivals(self):
        return zip(self.back, (2, 3, 1))

    def spread_end(self):
        for copy in self.back:
            copy.wait_recv()


class Ring:
    def __init__(self, place, wire, axis, quarter):
        self.place, self.wire, self.axis, self.quarter = place, wire, axis, quarter
        self.ahead, self.behind = place.ahead, place.behind
        self.to_ahead = place.peer(axis, self.ahead)
        self.to_behind = place.peer(axis, self.behind)

    def buffers(self, hop, near):
        self.hop, self.near = hop, near

    def order(self):
        return (2, self.behind)

    def send(self, block, by):
        src = block.at[self.rows(by)]
        if by is self.behind:
            self.got = [self.wire.send(src, self.near.at[1], self.to_behind)]
        else:
            self.far = self.wire.send(src, self.hop, self.to_ahead)

    def rows(self, by, base=0):
        start = base + self.place.step(self.axis, by) * self.quarter
        return pl.ds(pl.multiple_of(start, 8), self.quarter)

    def send_sum(self, block, more=0.0):
        self.far.wait_recv()
        self.hop[...] = (self.hop[...] + block[self.rows(self.ahead), :]) + more
        self.got.append(self.wire.send(self.hop, self.near.at[0], self.to_ahead))

    def result(self, block):
        for copy in self.got:
            copy.wait_recv()
        return block[self.rows(0), :] + self.near[0] + self.near[1]

    def spread(self, out, base):
        w = self.wire
        view = out.at[self.rows(0, base)]
        self.first = w.send(view, view, self.to_ahead)
        self.others = [w.send(view, view, self.to_behind)]

    def spread_on(self, out, base):
        self.first.wait_recv()
        view = out.at[self.rows(self.behind, base)]
        self.others.append(self.wire.send(view, view, self.to_ahead))

    def arrivals(self):
        return zip(self.others, (self.ahead, 2))

    def spread_end(self):
        for copy in self.others:
            copy.wait_recv()


class Part:
    def __init__(self, place, wire, tiles, axes, kind, before, g, out, bufs):
        self.place, self.wire, self.axes, self.g, self.out = place, wire, axes, g, out
        t, b = tiles, before
        self.t, self.b = t, b
        base, core = 256 * b, place.core
        self.mine = pl.multiple_of(base + core * (128 * t), 8)
        self.other = pl.multiple_of(base + (1 - core) * (128 * t), 8)
        self.at1 = self.mine + place.at[axes[0]] * (32 * t)
        self.at2 = self.at1 + place.at[axes[1]] * (8 * t)
        own, hop1, near1, t1, hop2, near2, last = bufs
        self.own_all = own
        self.own = own.at[self.spot(128)]
        self.t1 = t1.at[self.spot(32)]
        self.last = last.at[:, self.spot(8)]
        self.phase1 = (Ring if kind[0] == "r" else Quarters)(place, wire, axes[0], 32 * t)
        self.phase1.buffers(hop1.at[self.spot(32)], near1.at[:, self.spot(32)])
        self.phase2 = (Ring if kind[1] == "r" else Quarters)(place, wire, axes[1], 8 * t)
        self.phase2.buffers(hop2.at[self.spot(8)], near2.at[:, self.spot(8)])
        self.whole = kind[2] == "w"
        self.at = 0
        self.steps = [self.swap, self.join]
        if kind[0] == "r":
            self.steps.append(self.sums)
        self.steps.append(self.second)
        if kind[1] == "r":
            self.steps.append(self.second_sums)
        self.steps.append(self.third)
        if not self.whole:
            self.steps.append(self.third_again)
        self.steps.append(self.total)
        if kind[1] == "r":
            self.steps.append(self.back2_on)
        self.steps.append(self.back1)
        if kind[0] == "r":
            self.steps.append(self.back1_on)
        self.steps += [self.give_rest, self.taken]

    def advance(self):
        self.steps[self.at]()
        self.at += 1

    def spot(self, rows):
        return pl.ds(rows * self.b, rows * self.t)

    def swap(self):
        src = self.g.at[pl.ds(self.other, 128 * self.t)]
        self.swapped = self.wire.send(src, self.own, self.place.peer("core", 1))

    def add_quarter(self, by):
        rows = 32 * self.t
        start = self.place.step(self.axes[0], by) * rows
        to = pl.ds(pl.multiple_of(128 * self.b + start, 8), rows)
        mine = pl.ds(pl.multiple_of(self.mine + start, 8), rows)
        self.own_all[to, :] = self.own_all[to, :] + self.g[mine, :]

    def join(self):
        self.swapped.wait_recv()
        for by in self.phase1.order():
            self.add_quarter(by)
            self.phase1.send(self.own, by)

    def rest(self, by):
        start = self.place.step(self.axes[0], by) * (32 * self.t)
        return self.g[pl.ds(pl.multiple_of(self.mine + start, 8), 32 * self.t), :]

    def sums(self):
        self.phase1.send_sum(self.own, self.rest(self.place.ahead))

    def second(self):
        self.t1[...] = self.phase1.result(self.own) + self.rest(0)
        for by in self.phase2.order():
            self.phase2.send(self.t1, by)

    def second_sums(self):
        self.phase2.send_sum(self.t1)

    def third(self):
        axis = self.axes[2]
        value = self.phase2.result(self.t1)
        if self.whole:
            here = self.place.at[axis]
            self.last[here] = value
            view = self.last.at[here]
            self.thirds = [
                self.wire.send(view, view, self.place.peer(axis, by)) for by in (2, 1, 3)
            ]
        else:
            self.last[0] = value
            to = self.place.peer(axis, self.place.turns[axis][0])
            self.thirds = [self.wire.send(self.last.at[0], self.last.at[1], to)]

    def third_again(self):
        self.thirds[0].wait_recv()
        self.last[2] = self.last[0] + self.last[1]
        to = self.place.peer(self.axes[2], self.place.turns[self.axes[2]][1])
        self.thirds = [self.wire.send(self.last.at[2], self.last.at[3], to)]

    def total(self):
        for copy in self.thirds:
            copy.wait_recv()
        z = self.last
        rows = pl.ds(pl.multiple_of(self.at2, 8), 8 * self.t)
        if self.whole:
            self.out[rows, :] = (z[0] + z[1]) + (z[2] + z[3])
        else:
            self.out[rows, :] = z[2] + z[3]
        self.phase2.spread(self.out, self.at1)

    def back2_on(self):
        self.phase2.spread_on(self.out, self.at1)

    def back1(self):
        self.phase2.spread_end()
        self.phase1.spread(self.out, self.mine)
        self.given = []
        self.give(0)

    def back1_on(self):
        self.phase1.spread_on(self.out, self.mine)
        self.give(self.place.behind)

    def give(self, by):
        view = self.out.at[self.phase1.rows(by, self.mine)]
        self.given.append(self.wire.send(view, view, self.place.peer("core", 1)))

    def give_rest(self):
        for copy, by in self.phase1.arrivals():
            copy.wait_recv()
            self.give(by)

    def taken(self):
        for copy in self.given:
            copy.wait_recv()


def finish_kernel(
    acts,
    sgrads,
    out,
    acts_out,
    sg_out,
    gains,
    shifts,
    qkv_out,
    out_out,
    bout,
    up_out,
    bup,
    down_out,
    bdown,
    qkv,
    out_w,
    up,
    down,
    sems,
):
    copies = []

    def start(src, dst):
        copies.append(pltpu.make_async_copy(src, dst, sems.at[len(copies)]))
        copies[-1].start()

    start(acts, acts_out)
    start(sgrads, sg_out)
    for l in range(LAYERS):
        for kind, target, result, width in (
            ("qkv", qkv, qkv_out, 3 * INNER),
            ("out", out_w, out_out, INNER),
            ("up", up, up_out, FF),
            ("down", down, down_out, FF),
        ):
            for j in range(pl.cdiv(width, 128)):
                take = min(128, width - 128 * j)
                at = ROWS[l, kind, j]
                target[l, :, 128 * j : 128 * j + take] = out[at : at + COL, 0:take]
            start(target.at[l], result.at[l])
    write_small(out, gains, shifts, bout, bup, bdown)
    for copy in copies:
        copy.wait()


def finish(acts, sgrads, out):
    vmem = pl.BlockSpec(memory_space=pltpu.VMEM)
    hbm = pl.BlockSpec(memory_space=pl.ANY)

    def shape(*dims):
        return jax.ShapeDtypeStruct(dims, F32)

    return pl.pallas_call(
        finish_kernel,
        out_shape=(
            shape(8, D, SLOTS),
            shape(8, D, SLOTS),
            shape(LAYERS, 2, D),
            shape(LAYERS, 2, D),
            shape(LAYERS, D, 3 * INNER),
            shape(LAYERS, D, INNER),
            shape(LAYERS, D),
            shape(LAYERS, D, FF),
            shape(LAYERS, FF),
            shape(LAYERS, D, FF),
            shape(LAYERS, D),
        ),
        in_specs=[vmem, vmem, vmem],
        out_specs=(hbm, hbm, vmem, vmem, hbm, hbm, vmem, hbm, vmem, hbm, vmem),
        scratch_shapes=[
            pltpu.VMEM((LAYERS, D, 3 * INNER), F32),
            pltpu.VMEM((LAYERS, D, INNER), F32),
            pltpu.VMEM((LAYERS, D, FF), F32),
            pltpu.VMEM((LAYERS, D, FF), F32),
            pltpu.SemaphoreType.DMA((2 + 4 * LAYERS,)),
        ],
        compiler_params=pltpu.CompilerParams(vmem_limit_bytes=24 * 1024 * 1024),
        name="finish",
    )(acts, sgrads, out)


def write_small(out, gains, shifts, bout, bup, bdown):
    for l in range(LAYERS):

        def row(at, width):
            start = SMALL_ROW[l] + at
            rows = [out[start + j : start + j + 1, :] for j in range(pl.cdiv(width, 128))]
            return jnp.concatenate(rows, axis=1)[:, 0:width]

        for j in range(2):
            gains[l, j : j + 1, :] = row(7 + 2 * j, D)
            shifts[l, j : j + 1, :] = row(11 + 2 * j, D)
        bout[l : l + 1, :] = row(15, D)
        bup[l : l + 1, :] = row(0, FF)
        bdown[l : l + 1, :] = row(17, D)


def body(
    inputs,
    lengths,
    gene_mask,
    out_grad,
    gain,
    bias,
    wqkv,
    wout,
    bout,
    feats,
    wup,
    bup,
    wdown,
    bdown,
):
    def flip(value):
        return jnp.swapaxes(value, -1, -2)

    streams_and_sums = layers(
        (
            flip(inputs),
            lengths,
            gene_mask,
            flip(out_grad),
            gain,
            bias,
            wqkv,
            flip(wout),
            bout,
            feats,
            wup,
            bup,
            flip(wdown),
            bdown,
        )
    )
    acts, sgrads, gains, shifts, qkv, out, dbout, up, dbup, down, dbdown = finish(*streams_and_sums)
    return (
        flip(acts)[None],
        flip(sgrads)[None],
        gains,
        shifts,
        qkv,
        flip(out),
        dbout,
        up,
        dbup,
        flip(down),
        dbdown,
    )


def solution(mesh):
    placed = (
        P("dp", None, None),
        P("dp"),
        P("dp", None),
        P("dp", None, None),
    ) + (P(),) * 10
    return jax.shard_map(
        body,
        mesh=mesh,
        in_specs=placed,
        out_specs=(P("section", "dp", None, None),) * 2 + (P(),) * 9,
        check_vma=False,
    )
```
